32 devices in a mesh: frame: 8 (over z, x), strip: 4 (over y, core).
Axes of the slice: x: 2, y: 2, z: 4, core: 2. Of those that a mesh axis runs over, the one named last changes fastest.
Arguments:
- features: bfloat16 [8, 120, 32, 256], P('frame', None, 'strip'), may hold values from -6 to 6
- w_mutual: bfloat16 [2, 120, 360], replicated, may hold values from -4 to 4
- w_self: bfloat16 [2, 120, 360], replicated, may hold values from -4 to 4
- w_proj: bfloat16 [2, 240, 120], replicated, may hold values from -0.375 to 0.375
- w_gate: bfloat16 [2, 120, 240], replicated, may hold values from -0.5 to 0.5
- w_up: bfloat16 [2, 120, 240], replicated, may hold values from -0.5 to 0.5
- w_down: bfloat16 [2, 240, 120], replicated, may hold values from -0.375 to 0.375
Outputs:
- refined: bfloat16 [8, 120, 32, 256], P('frame', None, 'strip')
The draws below stay inside these ranges and needn't reach their ends.
All inputs are finite; a program needn't handle non-finite values.
Results may differ from the reference program's by a relative error of at most 0.012.
The reference program's roundings to bfloat16 on the way count: a program that leaves them out, or rounds other values in their place, can miss the bound.
Values may be sent and summed in bfloat16 or wider, within the bound.
A program may use at most 64 MiB of HBM per device.

```python
import jax
import jax.numpy as jnp
from jax import lax

C = 120
HEADS = 6
HEAD = 20
FFN = 240
WIN = 8
LAYERS = 2
COLS = 256
FRAMES = 8
NR = 32


def draw_features(key, part):
    key = jax.random.fold_in(key, 11)
    full_shape = (FRAMES, C, NR, COLS)
    values = jax.random.normal(key, full_shape, jnp.float32)
    return jnp.clip(values, -6.0, 6.0).astype(jnp.bfloat16)


def attention_weights(key, gain_lo, gain_hi):
    base_draw = jnp.clip(jax.random.normal(jax.random.fold_in(key, 1), (LAYERS, C, 3 * C), jnp.float32), -4.0, 4.0) * C ** (-0.5)
    head_gains = jnp.exp(jax.random.uniform(jax.random.fold_in(key, 2), (LAYERS, 1, HEADS), jnp.float32, jnp.log(gain_lo), jnp.log(gain_hi)))
    head_gains = jnp.repeat(head_gains, HEAD, axis=2)
    queries = base_draw[:, :, :C] * head_gains
    keys_part = base_draw[:, :, C:2 * C] * head_gains
    joined = jnp.concatenate([queries, keys_part, base_draw[:, :, 2 * C:]], axis=2)
    return jnp.clip(joined, -4.0, 4.0).astype(jnp.bfloat16)


def draw_w_mutual(key, part):
    key = jax.random.fold_in(key, 21)
    return attention_weights(key, 1.0, 1.0)


def draw_w_self(key, part):
    key = jax.random.fold_in(key, 31)
    return attention_weights(key, 1.0, 1.0)


def bell_draw(own_key, shape, width, most, held_as=jnp.bfloat16):
    values = width * jax.random.normal(own_key, shape, jnp.float32)
    return jnp.clip(values, min=-most, max=most).astype(held_as)


def setup_inputs(seed: int = 0) -> dict:
    splits = jax.random.split(jax.random.key(seed), 8)
    features = draw_features(jax.random.fold_in(splits[7], 71), 0)
    w_mutual = draw_w_mutual(jax.random.fold_in(splits[7], 71), 0)
    w_self = draw_w_self(jax.random.fold_in(splits[7], 71), 0)
    w_proj = bell_draw(splits[3], (LAYERS, 2 * C, C), (2 * C) ** -0.5, 0.375)
    w_gate = bell_draw(splits[4], (LAYERS, C, FFN), C ** -0.5, 0.5)
    w_up = bell_draw(splits[5], (LAYERS, C, FFN), C ** -0.5, 0.5)
    w_down = bell_draw(splits[6], (LAYERS, FFN, C), FFN ** -0.5, 0.375)
    return {"features": features, "w_mutual": w_mutual, "w_self": w_self, "w_proj": w_proj, "w_gate": w_gate, "w_up": w_up, "w_down": w_down}


epsilon = 1e-05
block_cols = 64

def normed(values):
    centre_mean = lax.optimization_barrier(jnp.mean(values, axis=0, keepdims=True))
    centred = values - centre_mean
    spread = lax.optimization_barrier(jnp.mean(centred * centred, axis=0, keepdims=True))
    return (centred * lax.rsqrt(spread + epsilon)).astype(jnp.bfloat16)

def project(weight, values):
    return jnp.einsum('ck,crw->krw', weight.astype(jnp.float32), values.astype(jnp.float32))

def to_windows(strip_data):
    win_count = strip_data.shape[2] // WIN
    shaped = strip_data.reshape(HEADS, HEAD, WIN, win_count, WIN)
    return shaped.transpose(3, 0, 2, 4, 1).reshape(win_count, HEADS, WIN * WIN, HEAD)

def from_windows(mixed_out):
    win_count = mixed_out.shape[0]
    shaped = mixed_out.reshape(win_count, HEADS, WIN, WIN, HEAD)
    return shaped.transpose(1, 4, 2, 0, 3).reshape(HEADS * HEAD, WIN, win_count * WIN)

def window_mix(queries, key_rows, values):
    scores = jnp.einsum('nhqd,nhkd->nhqk', queries.astype(jnp.float32), key_rows.astype(jnp.float32)) * HEAD ** (-0.5)
    row_max = lax.optimization_barrier(jnp.max(scores, axis=-1, keepdims=True))
    weights = jnp.exp(scores - row_max)
    weights = (weights / lax.optimization_barrier(jnp.sum(weights, axis=-1, keepdims=True))).astype(jnp.bfloat16)
    return jnp.einsum('nhqk,nhkd->nhqd', weights.astype(jnp.float32), values.astype(jnp.float32)).astype(jnp.bfloat16)

def attend(own_mut, own_self, other_kv):
    block_count = own_mut.shape[2] // block_cols

    def column_block(position):
        col_start = position * block_cols

        def take_cols(array):
            return lax.dynamic_slice_in_dim(array, col_start, block_cols, 2)
        mutual = window_mix(to_windows(take_cols(own_mut[:C])), to_windows(take_cols(other_kv[:C])), to_windows(take_cols(other_kv[C:2 * C])))
        key_rows = jnp.concatenate([to_windows(take_cols(own_self[C:2 * C])), to_windows(take_cols(other_kv[2 * C:3 * C]))], axis=2)
        value_rows = jnp.concatenate([to_windows(take_cols(own_self[2 * C:])), to_windows(take_cols(other_kv[3 * C:]))], axis=2)
        selfish = window_mix(to_windows(take_cols(own_self[:C])), key_rows, value_rows)
        return jnp.concatenate([from_windows(mutual), from_windows(selfish)], axis=0)
    blocks = lax.map(column_block, jnp.arange(block_count, dtype=jnp.int32))
    return blocks.transpose(1, 2, 0, 3).reshape(2 * C, WIN, block_count * block_cols)

def project_all(current, w_mut, w_slf):
    normal_rows = normed(current.astype(jnp.float32))
    return (normal_rows, project(w_mut, normal_rows).astype(jnp.bfloat16), project(w_slf, normal_rows).astype(jnp.bfloat16))

def finish(current, own_mut, own_self, other_kv, w_prj, w_gte, w_upp, w_dwn):
    joined = attend(own_mut, own_self, other_kv)
    middle = current.astype(jnp.float32) + project(w_prj, joined)
    second_norm = normed(middle)
    hidden = (jax.nn.gelu(project(w_gte, second_norm), approximate=False) * project(w_upp, second_norm)).astype(jnp.bfloat16)
    return (middle + project(w_dwn, hidden)).astype(jnp.bfloat16)

def pair_layer(frames, w_mut, w_slf, w_prj, w_gte, w_upp, w_dwn):
    frame_count, channels, band_rows, columns = frames.shape
    grouped = frames.reshape(frame_count // 2, 2, channels, band_rows // WIN, WIN, columns)
    grouped = grouped.transpose(0, 3, 1, 2, 4, 5).reshape(-1, 2, channels, WIN, columns)

    def pair_block(pair_frames):
        first_norm, first_mut, first_self = project_all(pair_frames[0], w_mut, w_slf)
        second_norm, second_mut, second_self = project_all(pair_frames[1], w_mut, w_slf)
        first_kv = jnp.concatenate([first_mut[C:], first_self[C:]], axis=0)
        second_kv = jnp.concatenate([second_mut[C:], second_self[C:]], axis=0)
        first_out = finish(pair_frames[0], first_mut, first_self, second_kv, w_prj, w_gte, w_upp, w_dwn)
        second_out = finish(pair_frames[1], second_mut, second_self, first_kv, w_prj, w_gte, w_upp, w_dwn)
        return jnp.stack([first_out, second_out])
    results = lax.map(pair_block, grouped)
    results = results.reshape(frame_count // 2, band_rows // WIN, 2, channels, WIN, columns)
    return results.transpose(0, 2, 3, 1, 4, 5).reshape(frame_count, channels, band_rows, columns)

def reference(features, w_mutual, w_self, w_proj, w_gate, w_up, w_down):
    half_win = WIN // 2
    layer_one = pair_layer(features, w_mutual[0], w_self[0], w_proj[0], w_gate[0], w_up[0], w_down[0])
    shifted = jnp.roll(layer_one, (-1, -half_win, -half_win), axis=(0, 2, 3))
    layer_two = pair_layer(shifted, w_mutual[1], w_self[1], w_proj[1], w_gate[1], w_up[1], w_down[1])
    return jnp.roll(layer_two, (1, half_win, half_win), axis=(0, 2, 3))
```

```python
import math

import jax
import jax.numpy as jnp
from jax import lax
from jax.experimental import pallas as pl
from jax.experimental.pallas import tpu as pltpu
from jax.sharding import PartitionSpec as P

C = 120
HEADS = 6
HEAD = 20
FFN = 240
WIN = 8
TOK = WIN * WIN
LANES = 128
PAIR = 2 * HEAD
GROUP = 48
VROWS = 3 * GROUP
CHUNK = 64
epsilon = 1e-05
f32 = jnp.float32
bf16 = jnp.bfloat16


def nn(a, b):
    return lax.dot_general(a, b, (((1,), (0,)), ((), ())), preferred_element_type=f32)


def nt(a, b):
    return lax.dot_general(a, b, (((1,), (1,)), ((), ())), preferred_element_type=f32)


def normed(values, axis):
    centred = values - jnp.mean(values, axis=axis, keepdims=True)
    spread = jnp.mean(centred * centred, axis=axis, keepdims=True)
    return (centred * lax.rsqrt(spread + epsilon)).astype(bf16)


def window_tokens(block):
    wins = block.shape[1] // WIN
    shaped = block.astype(f32).reshape(WIN, wins, WIN, C)
    return shaped.transpose(1, 0, 2, 3).reshape(wins * TOK, C)


def gelu(values):
    return 0.5 * values * (1.0 + lax.erf(values * (0.5 ** 0.5)))


def layer_chunk(x_tok, p_tok, wq, wk, wv, wpm, wps, wgu, wd):
    tokens = x_tok.shape[0]
    own = normed(x_tok, 1)
    other = normed(p_tok, 1)
    q_t = nt(wq, own)
    k_own = nn(own, wk[:, LANES:]).astype(bf16)
    k_other = nn(other, wk).astype(bf16)
    v_own = nt(wv[VROWS:], own)
    v_other = nt(wv, other)

    low = lax.broadcasted_iota(jnp.int32, (1, LANES), 1) < TOK
    row = lax.broadcasted_iota(jnp.int32, (LANES, LANES), 0)
    lane = lax.broadcasted_iota(jnp.int32, (LANES, LANES), 1)
    head_of = jnp.where(lane < TOK, 0, 1)
    masks = jnp.concatenate(
        [
            ((row >= PAIR * j + HEAD * head_of) & (row < PAIR * j + HEAD * head_of + HEAD))
            .astype(f32).astype(bf16)
            for j in range(3)
        ],
        axis=1,
    )
    first_head = lax.broadcasted_iota(jnp.int32, (C, LANES), 0) % PAIR < HEAD
    factor = HEAD ** (-0.5) * math.log2(math.e)

    def score(keys, query):
        return nn(keys, jnp.concatenate([query.astype(bf16)] * 3, axis=1) * masks)

    def soften(scores):
        top = jnp.max(scores, axis=0, keepdims=True)
        weights = jnp.exp2((scores - top) * factor)
        return (weights * (1.0 / jnp.sum(weights, axis=0, keepdims=True))).astype(bf16)

    def gather(values, weights):
        parts = [
            nn(values[GROUP * j : GROUP * (j + 1)], weights[:, LANES * j : LANES * (j + 1)])
            for j in range(3)
        ]
        return jnp.concatenate([part[:PAIR] for part in parts], axis=0)

    def swap(block):
        return pltpu.roll(block, TOK, 1)

    def merge(first, second):
        return jnp.where(
            first_head,
            jnp.where(low, first, swap(second)),
            jnp.where(low, swap(first), second),
        ).astype(bf16)

    def scores_of(pair):
        cols = slice(LANES * pair, LANES * (pair + 1))
        rows_a = slice(LANES * pair, LANES * pair + TOK)
        rows_b = slice(LANES * pair + TOK, LANES * (pair + 1))
        q_m, q_s = q_t[:LANES, cols], q_t[LANES:, cols]
        q_m_r, q_s_r = swap(q_m), swap(q_s)
        return [
            score(k_other[rows_a, :LANES], jnp.where(low, q_m, q_m_r)),
            score(k_other[rows_b, :LANES], jnp.where(low, q_m_r, q_m)),
            score(
                jnp.concatenate([k_own[rows_a], k_other[rows_a, LANES:]], axis=0),
                jnp.where(low, q_s, q_s_r),
            ),
            score(
                jnp.concatenate([k_own[rows_b], k_other[rows_b, LANES:]], axis=0),
                jnp.where(low, q_s_r, q_s),
            ),
        ]

    def mixed(pair, weights):
        cols = slice(LANES * pair, LANES * (pair + 1))
        vo, vp_m, vp_s = v_own[:, cols], v_other[:VROWS, cols], v_other[VROWS:, cols]
        vo_r, vp_m_r, vp_s_r = swap(vo), swap(vp_m), swap(vp_s)
        mut_a = gather(vp_m[:, :TOK].astype(bf16), weights[0])
        mut_b = gather(vp_m_r[:, :TOK].astype(bf16), weights[1])
        self_a = gather(jnp.where(low, vo, vp_s_r).astype(bf16), weights[2])
        self_b = gather(jnp.where(low, vo_r, vp_s).astype(bf16), weights[3])
        return merge(mut_a, mut_b), merge(self_a, self_b)

    pairs = tokens // LANES
    scores, weights, mutual, selfish = {}, {}, [], []
    for step in range(pairs + 2):
        if step < pairs:
            scores[step] = scores_of(step)
        if 0 <= step - 1 < pairs:
            weights[step - 1] = [soften(one) for one in scores.pop(step - 1)]
        if step >= 2:
            first, second = mixed(step - 2, weights.pop(step - 2))
            mutual.append(first)
            selfish.append(second)
    mutual = jnp.concatenate(mutual, axis=1)
    selfish = jnp.concatenate(selfish, axis=1)

    eye = (
        lax.broadcasted_iota(jnp.int32, (C, C), 0) == lax.broadcasted_iota(jnp.int32, (C, C), 1)
    ).astype(f32).astype(bf16)
    middle = nt(eye, x_tok.astype(bf16)) + (nn(wpm, mutual) + nn(wps, selfish))
    second = normed(middle, 0)
    gate_up = nn(wgu, second)
    hidden = (gelu(gate_up[:FFN]) * gate_up[FFN:]).astype(bf16)
    return middle + nn(wd, hidden)


def layer_result(x_tok, p_tok, layer, wq, wk, wv, wpm, wps, wgu, wd):
    result = layer_chunk(
        x_tok, p_tok, wq[layer], wk[layer], wv[layer], wpm[layer], wps[layer], wgu[layer],
        wd[layer],
    )
    wins = CHUNK // WIN
    back = result.T.reshape(wins, WIN, WIN, C).transpose(1, 0, 2, 3)
    return back.reshape(WIN, CHUNK, C).astype(bf16)


def arrange_weights(layer, w_mut, w_slf, w_prj, w_gte, w_upp, w_dwn, wq, wk, wv, wpm, wps, wgu, wd):
    blank = jnp.zeros((LANES - C, C), f32)
    for part, source in enumerate((w_mut, w_slf)):
        whole = source[layer].astype(f32)
        turned = whole.T
        wq[layer, LANES * part : LANES * (part + 1)] = jnp.concatenate(
            [turned[:C], blank], axis=0
        ).astype(bf16)
        wk[layer, :, LANES * part : LANES * part + C] = whole[:, C : 2 * C].astype(bf16)
        rows = []
        for j in range(3):
            rows += [turned[2 * C + PAIR * j : 2 * C + PAIR * (j + 1)], blank]
        wv[layer, VROWS * part : VROWS * (part + 1)] = jnp.concatenate(rows, axis=0).astype(bf16)
    joint = w_prj[layer].astype(f32)
    wpm[layer] = joint[:C].T.astype(bf16)
    wps[layer] = joint[C:].T.astype(bf16)
    wgu[layer, :FFN] = w_gte[layer].astype(f32).T.astype(bf16)
    wgu[layer, FFN:] = w_upp[layer].astype(f32).T.astype(bf16)
    wd[layer] = w_dwn[layer].astype(f32).T.astype(bf16)


def both_layers(
    x_ref, w_mut, w_slf, w_prj, w_gte, w_upp, w_dwn, out_ref,
    partner, upper, lower, from_below, mate_lower, mate_upper, result_low,
    wq, wk, wv, wpm, wps, wgu, wd, send, recv,
):
    half = WIN // 2
    cols = x_ref.shape[1]
    chunks = cols // CHUNK
    wide = CHUNK + 16
    frames, strips = lax.axis_size("frame"), lax.axis_size("strip")
    f, s = lax.axis_index("frame"), lax.axis_index("strip")
    odd = lax.rem(f, 2)
    twin = f + 1 - 2 * odd
    mate = lax.rem(f + 2 * odd - 1 + frames, frames)
    above = lax.rem(s + strips - 1, strips)
    below = lax.rem(s + 1, strips)

    def span(c, width=CHUNK):
        return pl.ds(pl.multiple_of(c * CHUNK, CHUNK), width)

    def copy(group, c):
        source, target, device = (
            (x_ref, partner, (twin, s)),
            (upper, from_below, (f, above)),
            (lower, mate_lower, (mate, s)),
            (upper, mate_upper, (mate, above)),
            (result_low, out_ref, (f, below)),
        )[group]
        rows = pl.ds(0, WIN if group == 0 else half)
        return pltpu.make_async_remote_copy(
            src_ref=source.at[rows, span(c), :],
            dst_ref=target.at[rows, span(c), :],
            send_sem=send.at[group, c],
            recv_sem=recv.at[group, c],
            device_id=device,
            device_id_type=pl.DeviceIdType.MESH,
        )

    barrier = pltpu.get_barrier_semaphore()
    known = [(twin, s), (mate, s), (f, above), (f, below), (mate, above), (mate, below)]
    for device in known:
        pl.semaphore_signal(
            barrier, inc=1, device_id=device, device_id_type=pl.DeviceIdType.MESH
        )
    pl.semaphore_wait(barrier, len(known))
    for c in range(chunks):
        copy(0, c).start()

    wk[...] = jnp.zeros_like(wk)
    raw = (w_mut, w_slf, w_prj, w_gte, w_upp, w_dwn)
    ready = (wq, wk, wv, wpm, wps, wgu, wd)
    for layer in range(2):
        arrange_weights(layer, *raw, *ready)

    @pl.loop(0, chunks)
    def _(c):
        copy(0, c).wait_recv()
        here = layer_result(
            window_tokens(x_ref[:, span(c), :]), window_tokens(partner[:, span(c), :]), 0, *ready
        )
        upper[:, span(c), :] = here[:half]
        lower[:, span(c), :] = here[half:]
        for group in (2, 3, 1):
            copy(group, c).start()

    for group in (2, 3, 1):
        copy(group, 0).wait_recv()
    for held in (lower, from_below, mate_lower, mate_upper):
        held[:, cols : cols + 16, :] = held[:, :16, :]

    def shifted(top, bottom, c):
        joined = jnp.concatenate([top[:, span(c, wide), :], bottom[:, span(c, wide), :]], axis=0)
        return window_tokens(joined.astype(f32)[:, half : half + CHUNK, :])

    @pl.loop(0, chunks)
    def _(c):
        @pl.when(c < chunks - 1)
        def _():
            for group in (2, 3, 1):
                copy(group, c + 1).wait_recv()

        here = layer_result(
            shifted(lower, from_below, c), shifted(mate_lower, mate_upper, c), 1, *ready
        )
        out_ref[half:, span(c), :] = here[:half]
        result_low[:, span(c), :] = here[half:]
        copy(4, c).start()

    for c in range(chunks):
        copy(4, c).wait_recv()
        for group in range(5):
            copy(group, c).wait_send()


def on_device(features, w_mutual, w_self, w_proj, w_gate, w_up, w_down):
    half = WIN // 2
    current = features[0].transpose(1, 2, 0)
    cols = current.shape[1]
    chunks = cols // CHUNK
    held = pltpu.VMEM((half, cols + 16, C), bf16)
    plain = pltpu.VMEM((half, cols, C), bf16)
    in_vmem = pl.BlockSpec(memory_space=pltpu.VMEM)
    result = pl.pallas_call(
        both_layers,
        in_specs=[in_vmem] * 7,
        out_specs=in_vmem,
        out_shape=jax.ShapeDtypeStruct(current.shape, bf16),
        scratch_shapes=[
            pltpu.VMEM((WIN, cols, C), bf16),
            plain,
            held,
            held,
            held,
            held,
            plain,
            pltpu.VMEM((2, 2 * LANES, C), bf16),
            pltpu.VMEM((2, C, 2 * LANES), bf16),
            pltpu.VMEM((2, 2 * VROWS, C), bf16),
            pltpu.VMEM((2, C, C), bf16),
            pltpu.VMEM((2, C, C), bf16),
            pltpu.VMEM((2, 2 * FFN, C), bf16),
            pltpu.VMEM((2, C, FFN), bf16),
            pltpu.SemaphoreType.DMA((5, chunks)),
            pltpu.SemaphoreType.DMA((5, chunks)),
        ],
        compiler_params=pltpu.CompilerParams(
            vmem_limit_bytes=48 * 1024 * 1024, collective_id=0, has_side_effects=True
        ),
        cost_estimate=pl.CostEstimate(
            flops=2_400_000_000, bytes_accessed=3_000_000, transcendentals=6_000_000
        ),
    )(current, w_mutual, w_self, w_proj, w_gate, w_up, w_down)
    return jnp.roll(result, half, axis=1).transpose(2, 0, 1)[None]


def solution(mesh):
    in_specs = (P("frame", None, "strip", None), P(), P(), P(), P(), P(), P())
    out_specs = P("frame", None, "strip", None)
    return jax.shard_map(
        on_device, mesh=mesh, in_specs=in_specs, out_specs=out_specs, check_vma=False
    )
```

```python
import math

import jax
import jax.numpy as jnp
from jax import lax
from jax.experimental import pallas as pl
from jax.experimental.pallas import tpu as pltpu
from jax.sharding import PartitionSpec as P

C = 120
HEADS = 6
HEAD = 20
FFN = 240
WIN = 8
TOK = WIN * WIN
LANES = 128
PAIR = 2 * HEAD
GROUP = 48
VROWS = 3 * GROUP
CHUNK = 32
SLACK = 16
epsilon = 1e-05
f32 = jnp.float32
bf16 = jnp.bfloat16


def nn(a, b):
    return lax.dot_general(a, b, (((1,), (0,)), ((), ())), preferred_element_type=f32)


def nt(a, b):
    return lax.dot_general(a, b, (((1,), (1,)), ((), ())), preferred_element_type=f32)


def normed(values, axis):
    centred = values - jnp.mean(values, axis=axis, keepdims=True)
    spread = jnp.mean(centred * centred, axis=axis, keepdims=True)
    return (centred * lax.rsqrt(spread + epsilon)).astype(bf16)


def window_tokens(block):
    wins = block.shape[1] // WIN
    shaped = block.astype(f32).reshape(WIN, wins, WIN, C)
    return shaped.transpose(1, 0, 2, 3).reshape(wins * TOK, C)


def gelu(values):
    return 0.5 * values * (1.0 + lax.erf(values * (0.5 ** 0.5)))


def layer_chunk(x_tok, wq, wk, wv, wpm, wps, wgu, wd):
    tokens = x_tok.shape[0]
    normal = normed(x_tok, 1)
    q_t = nt(wq, normal)
    keys = nn(normal, wk).astype(bf16)
    values = nt(wv, normal)
    pairs = tokens // LANES

    low = lax.broadcasted_iota(jnp.int32, (1, LANES), 1) < TOK
    row = lax.broadcasted_iota(jnp.int32, (LANES, LANES), 0)
    lane = lax.broadcasted_iota(jnp.int32, (LANES, LANES), 1)
    head_of = jnp.where(lane < TOK, 0, 1)
    masks = jnp.concatenate(
        [
            ((row >= PAIR * j + HEAD * head_of) & (row < PAIR * j + HEAD * head_of + HEAD))
            .astype(f32).astype(bf16)
            for j in range(3)
        ],
        axis=1,
    )
    first_head = lax.broadcasted_iota(jnp.int32, (C, LANES), 0) % PAIR < HEAD
    factor = HEAD ** (-0.5) * math.log2(math.e)

    def score(key_rows, query):
        return nn(key_rows, jnp.concatenate([query.astype(bf16)] * 3, axis=1) * masks)

    def soften(scores):
        top = jnp.max(scores, axis=0, keepdims=True)
        weights = jnp.exp2((scores - top) * factor)
        return (weights * (1.0 / jnp.sum(weights, axis=0, keepdims=True))).astype(bf16)

    def gather(value_rows, weights):
        parts = [
            nn(value_rows[GROUP * j : GROUP * (j + 1)], weights[:, LANES * j : LANES * (j + 1)])
            for j in range(3)
        ]
        return jnp.concatenate([part[:PAIR] for part in parts], axis=0)

    def swap(block):
        return pltpu.roll(block, TOK, 1)

    def merge(first, second):
        return jnp.where(
            first_head,
            jnp.where(low, first, swap(second)),
            jnp.where(low, swap(first), second),
        ).astype(bf16)

    def scores_of(pair):
        mate = (pair + pairs // 2) % pairs
        cols = slice(LANES * pair, LANES * (pair + 1))
        own_a = slice(LANES * pair, LANES * pair + TOK)
        own_b = slice(LANES * pair + TOK, LANES * (pair + 1))
        mate_a = slice(LANES * mate, LANES * mate + TOK)
        mate_b = slice(LANES * mate + TOK, LANES * (mate + 1))
        q_m, q_s = q_t[:LANES, cols], q_t[LANES:, cols]
        q_m_r, q_s_r = swap(q_m), swap(q_s)
        return [
            score(keys[mate_a, :LANES], jnp.where(low, q_m, q_m_r)),
            score(keys[mate_b, :LANES], jnp.where(low, q_m_r, q_m)),
            score(
                jnp.concatenate([keys[own_a, LANES:], keys[mate_a, LANES:]], axis=0),
                jnp.where(low, q_s, q_s_r),
            ),
            score(
                jnp.concatenate([keys[own_b, LANES:], keys[mate_b, LANES:]], axis=0),
                jnp.where(low, q_s_r, q_s),
            ),
        ]

    def mixed(pair, weights):
        mate = (pair + pairs // 2) % pairs
        cols = slice(LANES * pair, LANES * (pair + 1))
        mate_cols = slice(LANES * mate, LANES * (mate + 1))
        v_own, v_m, v_s = values[VROWS:, cols], values[:VROWS, mate_cols], values[VROWS:, mate_cols]
        mut_a = gather(v_m[:, :TOK].astype(bf16), weights[0])
        mut_b = gather(swap(v_m)[:, :TOK].astype(bf16), weights[1])
        self_a = gather(jnp.where(low, v_own, swap(v_s)).astype(bf16), weights[2])
        self_b = gather(jnp.where(low, swap(v_own), v_s).astype(bf16), weights[3])
        return merge(mut_a, mut_b), merge(self_a, self_b)

    scores, weights, mutual, selfish = {}, {}, [], []
    for step in range(pairs + 2):
        if step < pairs:
            scores[step] = scores_of(step)
        if 0 <= step - 1 < pairs:
            weights[step - 1] = [soften(one) for one in scores.pop(step - 1)]
        if step >= 2:
            first, second = mixed(step - 2, weights.pop(step - 2))
            mutual.append(first)
            selfish.append(second)
    mutual = jnp.concatenate(mutual, axis=1)
    selfish = jnp.concatenate(selfish, axis=1)

    eye = (
        lax.broadcasted_iota(jnp.int32, (C, C), 0) == lax.broadcasted_iota(jnp.int32, (C, C), 1)
    ).astype(f32).astype(bf16)
    middle = nt(eye, x_tok.astype(bf16)) + (nn(wpm, mutual) + nn(wps, selfish))
    second = normed(middle, 0)
    gate_up = nn(wgu, second)
    hidden = (gelu(gate_up[:FFN]) * gate_up[FFN:]).astype(bf16)
    return middle + nn(wd, hidden)


def layer_result(first, second, layer, wq, wk, wv, wpm, wps, wgu, wd):
    tokens = jnp.concatenate([window_tokens(first), window_tokens(second)], axis=0)
    result = layer_chunk(
        tokens, wq[layer], wk[layer], wv[layer], wpm[layer], wps[layer], wgu[layer], wd[layer]
    )
    wins = CHUNK // WIN
    back = result.T.reshape(2, wins, WIN, WIN, C).transpose(0, 2, 1, 3, 4)
    back = back.reshape(2, WIN, CHUNK, C).astype(bf16)
    return back[0], back[1]


def arrange_weights(layer, w_mut, w_slf, w_prj, w_gte, w_upp, w_dwn, wq, wk, wv, wpm, wps, wgu, wd):
    blank = jnp.zeros((LANES - C, C), f32)
    for part, source in enumerate((w_mut, w_slf)):
        whole = source[layer].astype(f32)
        turned = whole.T
        wq[layer, LANES * part : LANES * (part + 1)] = jnp.concatenate(
            [turned[:C], blank], axis=0
        ).astype(bf16)
        wk[layer, :, LANES * part : LANES * part + C] = whole[:, C : 2 * C].astype(bf16)
        rows = []
        for j in range(3):
            rows += [turned[2 * C + PAIR * j : 2 * C + PAIR * (j + 1)], blank]
        wv[layer, VROWS * part : VROWS * (part + 1)] = jnp.concatenate(rows, axis=0).astype(bf16)
    joint = w_prj[layer].astype(f32)
    wpm[layer] = joint[:C].T.astype(bf16)
    wps[layer] = joint[C:].T.astype(bf16)
    wgu[layer, :FFN] = w_gte[layer].astype(f32).T.astype(bf16)
    wgu[layer, FFN:] = w_upp[layer].astype(f32).T.astype(bf16)
    wd[layer] = w_dwn[layer].astype(f32).T.astype(bf16)


def both_layers(
    x_ref, w_mut, w_slf, w_prj, w_gte, w_upp, w_dwn, out_ref,
    partner, upper, lower, halves, result,
    wq, wk, wv, wpm, wps, wgu, wd,
    send, recv, edge_send, edge_recv, out_send, out_recv,
):
    half = WIN // 2
    cols = x_ref.shape[1] // 2
    chunks = cols // CHUNK
    wide = CHUNK + SLACK
    couples, strips = lax.axis_size("frame") // 2, lax.axis_size("strip")
    f, s = lax.axis_index("frame"), lax.axis_index("strip")
    side = lax.rem(f, 2)
    couple = lax.div(f, 2)

    def at(d_couple, to_side, d_strip):
        to_couple = lax.rem(couple + d_couple + couples, couples)
        return (2 * to_couple + to_side, lax.rem(s + d_strip + strips, strips))

    def span(c, width=CHUNK):
        return pl.ds(pl.multiple_of(c * CHUNK, CHUNK), width)

    def place(c, which):
        return pl.ds(pl.multiple_of(which * cols + c * CHUNK, CHUNK), CHUNK)

    def remote(source, target, send_sem, recv_sem, device):
        return pltpu.make_async_remote_copy(
            src_ref=source,
            dst_ref=target,
            send_sem=send_sem,
            recv_sem=recv_sem,
            device_id=device,
            device_id_type=pl.DeviceIdType.MESH,
        )

    def copy(group, c):
        source, target, device = (
            (x_ref.at[:, place(c, 1 - side), :], partner.at[:, span(c), :], at(0, 1 - side, 0)),
            (upper.at[1, :, span(c), :], halves.at[1, :, span(c), :], at(0, side, -1)),
            (lower.at[0, :, span(c), :], halves.at[2, :, span(c), :], at(-1, side, 0)),
            (upper.at[0, :, span(c), :], halves.at[3, :, span(c), :], at(-1, side, -1)),
        )[group]
        return remote(source, target, send.at[group, c], recv.at[group, c], device)

    def edge(group):
        source, device = (
            (lower.at[1], at(0, 1 - side, 0)),
            (upper.at[1], at(0, 1 - side, -1)),
            (lower.at[0], at(-1, 1 - side, 0)),
            (upper.at[0], at(-1, 1 - side, -1)),
        )[group]
        return remote(
            source.at[:, pl.ds(0, SLACK), :],
            halves.at[group, :, pl.ds(cols, SLACK), :],
            edge_send.at[group],
            edge_recv.at[group],
            device,
        )

    def give_back(kind, c, origin):
        frame, part = kind // 2, kind % 2
        device = at(1 - frame, frame, part)
        return remote(
            result.at[1 - frame, pl.ds(half * part, half), span(c), :],
            out_ref.at[pl.ds(half * (1 - part), half), place(c, origin), :],
            out_send.at[kind, c],
            out_recv.at[part, origin, c],
            device,
        )

    barrier = pltpu.get_barrier_semaphore()
    known = [
        at(i, to_side, j)
        for i in (-1, 0, 1)
        for j in (-1, 0, 1)
        for to_side in ((1 - side,) if (i, j) == (0, 0) else (side, 1 - side))
    ]
    for device in known:
        pl.semaphore_signal(
            barrier, inc=1, device_id=device, device_id_type=pl.DeviceIdType.MESH
        )
    pl.semaphore_wait(barrier, len(known))

    copy(0, 0).start()
    wk[...] = jnp.zeros_like(wk)
    raw = (w_mut, w_slf, w_prj, w_gte, w_upp, w_dwn)
    ready = (wq, wk, wv, wpm, wps, wgu, wd)
    arrange_weights(0, *raw, *ready)
    for c in range(1, chunks):
        copy(0, c).start()
    arrange_weights(1, *raw, *ready)

    @pl.loop(0, chunks)
    def _(c):
        copy(0, c).wait_recv()
        own, other = layer_result(
            x_ref[:, place(c, side), :], partner[:, span(c), :], 0, *ready
        )
        upper[side, :, span(c), :] = own[:half]
        lower[side, :, span(c), :] = own[half:]
        upper[1 - side, :, span(c), :] = other[:half]
        lower[1 - side, :, span(c), :] = other[half:]
        for group in (2, 3, 1):
            copy(group, c).start()
        halves[0, :, span(c), :] = lower[1, :, span(c), :]

        @pl.when(c == 0)
        def _():
            for group in range(4):
                edge(group).start()

    for group in (2, 3, 1):
        copy(group, 0).wait_recv()

    def shifted(top, bottom, c):
        joined = jnp.concatenate(
            [halves[top, :, span(c, wide), :], halves[bottom, :, span(c, wide), :]], axis=0
        )
        return joined.astype(f32)[:, half : half + CHUNK, :]

    @pl.loop(0, chunks)
    def _(c):
        @pl.when(c < chunks - 1)
        def _():
            for group in (2, 3, 1):
                copy(group, c + 1).wait_recv()

        @pl.when(c == chunks - 1)
        def _():
            for group in range(4):
                edge(group).wait_recv()

        odd, even = layer_result(shifted(0, 1, c), shifted(2, 3, c), 1, *ready)
        result[0, :, span(c), :] = odd
        result[1, :, span(c), :] = even
        give_back(0, c, side).start()
        give_back(1, c, side).start()
        give_back(3, c, side).start()

        @pl.when(side == 0)
        def _():
            give_back(2, c, side).start()

        @pl.when(side == 1)
        def _():
            out_ref[half:, place(c, 1), :] = odd[:half]

    for c in range(chunks):
        give_back(0, c, 0).wait_recv()
        give_back(1, c, 0).wait_recv()
        give_back(1, c, 1).wait_recv()
        for kind in (0, 1, 3):
            give_back(kind, c, side).wait_send()
        for group in range(4):
            copy(group, c).wait_send()

    @pl.when(side == 0)
    def _():
        for c in range(chunks):
            give_back(0, c, 1).wait_recv()
            give_back(2, c, 0).wait_send()

    for group in range(4):
        edge(group).wait_send()


def on_device(features, w_mutual, w_self, w_proj, w_gate, w_up, w_down):
    half = WIN // 2
    current = features[0].transpose(1, 2, 0)
    cols = current.shape[1] // 2
    chunks = cols // CHUNK
    in_vmem = pl.BlockSpec(memory_space=pltpu.VMEM)
    result = pl.pallas_call(
        both_layers,
        in_specs=[in_vmem] * 7,
        out_specs=in_vmem,
        out_shape=jax.ShapeDtypeStruct(current.shape, bf16),
        scratch_shapes=[
            pltpu.VMEM((WIN, cols, C), bf16),
            pltpu.VMEM((2, half, cols, C), bf16),
            pltpu.VMEM((2, half, cols, C), bf16),
            pltpu.VMEM((4, half, cols + SLACK, C), bf16),
            pltpu.VMEM((2, WIN, cols, C), bf16),
            pltpu.VMEM((2, 2 * LANES, C), bf16),
            pltpu.VMEM((2, C, 2 * LANES), bf16),
            pltpu.VMEM((2, 2 * VROWS, C), bf16),
            pltpu.VMEM((2, C, C), bf16),
            pltpu.VMEM((2, C, C), bf16),
            pltpu.VMEM((2, 2 * FFN, C), bf16),
            pltpu.VMEM((2, C, FFN), bf16),
            pltpu.SemaphoreType.DMA((4, chunks)),
            pltpu.SemaphoreType.DMA((4, chunks)),
            pltpu.SemaphoreType.DMA((4,)),
            pltpu.SemaphoreType.DMA((4,)),
            pltpu.SemaphoreType.DMA((4, chunks)),
            pltpu.SemaphoreType.DMA((2, 2, chunks)),
        ],
        compiler_params=pltpu.CompilerParams(
            vmem_limit_bytes=48 * 1024 * 1024, collective_id=0, has_side_effects=True
        ),
        cost_estimate=pl.CostEstimate(
            flops=2_400_000_000, bytes_accessed=3_000_000, transcendentals=6_000_000
        ),
    )(current, w_mutual, w_self, w_proj, w_gate, w_up, w_down)
    return jnp.roll(result, half, axis=1).transpose(2, 0, 1)[None]


def solution(mesh):
    in_specs = (P("frame", None, "strip", None), P(), P(), P(), P(), P(), P())
    out_specs = P("frame", None, "strip", None)
    return jax.shard_map(
        on_device, mesh=mesh, in_specs=in_specs, out_specs=out_specs, check_vma=False
    )
```

```python
import math

import jax
import jax.numpy as jnp
from jax import lax
from jax.experimental import pallas as pl
from jax.experimental.pallas import tpu as pltpu
from jax.sharding import PartitionSpec as P

C = 120
HEADS = 6
HEAD = 20
FFN = 240
WIN = 8
TOK = WIN * WIN
LANES = 128
PAIR = 2 * HEAD
GROUP = 48
VROWS = 3 * GROUP
CHUNK = 32
SLACK = 16
epsilon = 1e-05
f32 = jnp.float32
bf16 = jnp.bfloat16


def nn(a, b):
    return lax.dot_general(a, b, (((1,), (0,)), ((), ())), preferred_element_type=f32)


def nt(a, b):
    return lax.dot_general(a, b, (((1,), (1,)), ((), ())), preferred_element_type=f32)


def normed(values, axis):
    centred = values - jnp.mean(values, axis=axis, keepdims=True)
    spread = jnp.mean(centred * centred, axis=axis, keepdims=True)
    return (centred * lax.rsqrt(spread + epsilon)).astype(bf16)


def window_tokens(block):
    wins = block.shape[1] // WIN
    shaped = block.astype(f32).reshape(WIN, wins, WIN, C)
    return shaped.transpose(1, 0, 2, 3).reshape(wins * TOK, C)


def gelu(values):
    return 0.5 * values * (1.0 + lax.erf(values * (0.5 ** 0.5)))


def layer_chunk(x_tok, wq, wk, wv, wpm, wps, wgu, wd):
    tokens = x_tok.shape[0]
    normal = normed(x_tok, 1)
    q_t = nt(wq, normal)
    keys = nn(normal, wk).astype(bf16)
    values = nt(wv, normal)
    pairs = tokens // LANES

    low = lax.broadcasted_iota(jnp.int32, (1, LANES), 1) < TOK
    row = lax.broadcasted_iota(jnp.int32, (LANES, LANES), 0)
    lane = lax.broadcasted_iota(jnp.int32, (LANES, LANES), 1)
    head_of = jnp.where(lane < TOK, 0, 1)
    masks = jnp.concatenate(
        [
            ((row >= PAIR * j + HEAD * head_of) & (row < PAIR * j + HEAD * head_of + HEAD))
            .astype(f32).astype(bf16)
            for j in range(3)
        ],
        axis=1,
    )
    first_head = lax.broadcasted_iota(jnp.int32, (C, LANES), 0) % PAIR < HEAD
    factor = HEAD ** (-0.5) * math.log2(math.e)

    def block_diagonal(first, second):
        right = jnp.zeros((first.shape[0], second.shape[1]), bf16)
        left = jnp.zeros((second.shape[0], first.shape[1]), bf16)
        return jnp.concatenate(
            [
                jnp.concatenate([first, right], axis=1),
                jnp.concatenate([left, second], axis=1),
            ],
            axis=0,
        )

    def spread(query):
        return jnp.concatenate([query.astype(bf16)] * 3, axis=1) * masks

    def score(own, mate, q_self, q_mut):
        self_keys = jnp.concatenate([keys[own, LANES:], keys[mate, LANES:]], axis=0)
        return nn(
            block_diagonal(self_keys, keys[mate, :LANES]),
            jnp.concatenate([spread(q_self), spread(q_mut)], axis=0),
        )

    def soften(scores):
        top = jnp.max(scores, axis=0, keepdims=True)
        weights = jnp.exp2((scores - top) * factor)
        return (weights * (1.0 / jnp.sum(weights, axis=0, keepdims=True))).astype(bf16)

    def soften_both(scores):
        return jnp.concatenate([soften(scores[: 2 * TOK]), soften(scores[2 * TOK :])], axis=0)

    def gather(v_self, v_mut, weights):
        parts = [
            nn(
                block_diagonal(
                    v_self[GROUP * j : GROUP * (j + 1)], v_mut[GROUP * j : GROUP * (j + 1)]
                ),
                weights[:, LANES * j : LANES * (j + 1)],
            )
            for j in range(3)
        ]
        selfish = jnp.concatenate([part[:PAIR] for part in parts], axis=0)
        return selfish, jnp.concatenate([part[GROUP : GROUP + PAIR] for part in parts], axis=0)

    def swap(block):
        return pltpu.roll(block, TOK, 1)

    def merge(first, second):
        return jnp.where(
            first_head,
            jnp.where(low, first, swap(second)),
            jnp.where(low, swap(first), second),
        ).astype(bf16)

    def scores_of(pair):
        mate = (pair + pairs // 2) % pairs
        cols = slice(LANES * pair, LANES * (pair + 1))
        own_a = slice(LANES * pair, LANES * pair + TOK)
        own_b = slice(LANES * pair + TOK, LANES * (pair + 1))
        mate_a = slice(LANES * mate, LANES * mate + TOK)
        mate_b = slice(LANES * mate + TOK, LANES * (mate + 1))
        q_m, q_s = q_t[:LANES, cols], q_t[LANES:, cols]
        q_m_r, q_s_r = swap(q_m), swap(q_s)
        return [
            score(own_a, mate_a, jnp.where(low, q_s, q_s_r), jnp.where(low, q_m, q_m_r)),
            score(own_b, mate_b, jnp.where(low, q_s_r, q_s), jnp.where(low, q_m_r, q_m)),
        ]

    def mixed(pair, weights):
        mate = (pair + pairs // 2) % pairs
        cols = slice(LANES * pair, LANES * (pair + 1))
        mate_cols = slice(LANES * mate, LANES * (mate + 1))
        v_own, v_m, v_s = values[VROWS:, cols], values[:VROWS, mate_cols], values[VROWS:, mate_cols]
        self_a, mut_a = gather(
            jnp.where(low, v_own, swap(v_s)).astype(bf16), v_m[:, :TOK].astype(bf16), weights[0]
        )
        self_b, mut_b = gather(
            jnp.where(low, swap(v_own), v_s).astype(bf16),
            swap(v_m)[:, :TOK].astype(bf16),
            weights[1],
        )
        return merge(mut_a, mut_b), merge(self_a, self_b)

    scores, weights, mutual, selfish = {}, {}, [], []
    for step in range(pairs + 2):
        if step < pairs:
            scores[step] = scores_of(step)
        if 0 <= step - 1 < pairs:
            weights[step - 1] = [soften_both(one) for one in scores.pop(step - 1)]
        if step >= 2:
            first, second = mixed(step - 2, weights.pop(step - 2))
            mutual.append(first)
            selfish.append(second)
    mutual = jnp.concatenate(mutual, axis=1)
    selfish = jnp.concatenate(selfish, axis=1)

    eye = (
        lax.broadcasted_iota(jnp.int32, (C, C), 0) == lax.broadcasted_iota(jnp.int32, (C, C), 1)
    ).astype(f32).astype(bf16)
    middle = nt(eye, x_tok.astype(bf16)) + (nn(wpm, mutual) + nn(wps, selfish))
    second = normed(middle, 0)
    gate_up = nn(wgu, second)
    hidden = (gelu(gate_up[:FFN]) * gate_up[FFN:]).astype(bf16)
    return middle + nn(wd, hidden)


def layer_result(first, second, layer, wq, wk, wv, wpm, wps, wgu, wd):
    tokens = jnp.concatenate([window_tokens(first), window_tokens(second)], axis=0)
    result = layer_chunk(
        tokens, wq[layer], wk[layer], wv[layer], wpm[layer], wps[layer], wgu[layer], wd[layer]
    )
    wins = CHUNK // WIN
    back = result.T.reshape(2, wins, WIN, WIN, C).transpose(0, 2, 1, 3, 4)
    back = back.reshape(2, WIN, CHUNK, C).astype(bf16)
    return back[0], back[1]


def arrange_weights(layer, w_mut, w_slf, w_prj, w_gte, w_upp, w_dwn, wq, wk, wv, wpm, wps, wgu, wd):
    blank = jnp.zeros((LANES - C, C), f32)
    for part, source in enumerate((w_mut, w_slf)):
        whole = source[layer].astype(f32)
        turned = whole.T
        wq[layer, LANES * part : LANES * (part + 1)] = jnp.concatenate(
            [turned[:C], blank], axis=0
        ).astype(bf16)
        wk[layer, :, LANES * part : LANES * part + C] = whole[:, C : 2 * C].astype(bf16)
        rows = []
        for j in range(3):
            rows += [turned[2 * C + PAIR * j : 2 * C + PAIR * (j + 1)], blank]
        wv[layer, VROWS * part : VROWS * (part + 1)] = jnp.concatenate(rows, axis=0).astype(bf16)
    joint = w_prj[layer].astype(f32)
    wpm[layer] = joint[:C].T.astype(bf16)
    wps[layer] = joint[C:].T.astype(bf16)
    wgu[layer, :FFN] = w_gte[layer].astype(f32).T.astype(bf16)
    wgu[layer, FFN:] = w_upp[layer].astype(f32).T.astype(bf16)
    wd[layer] = w_dwn[layer].astype(f32).T.astype(bf16)


def both_layers(
    x_ref, w_mut, w_slf, w_prj, w_gte, w_upp, w_dwn, out_ref,
    partner, upper, lower, halves, result,
    wq, wk, wv, wpm, wps, wgu, wd,
    send, recv, edge_send, edge_recv, out_send, out_recv,
):
    half = WIN // 2
    cols = x_ref.shape[1] // 2
    chunks = cols // CHUNK
    wide = CHUNK + SLACK
    couples, strips = lax.axis_size("frame") // 2, lax.axis_size("strip")
    f, s = lax.axis_index("frame"), lax.axis_index("strip")
    side = lax.rem(f, 2)
    couple = lax.div(f, 2)

    def at(d_couple, to_side, d_strip):
        to_couple = lax.rem(couple + d_couple + couples, couples)
        return (2 * to_couple + to_side, lax.rem(s + d_strip + strips, strips))

    def span(c, width=CHUNK):
        return pl.ds(pl.multiple_of(c * CHUNK, CHUNK), width)

    def place(c, which):
        return pl.ds(pl.multiple_of(which * cols + c * CHUNK, CHUNK), CHUNK)

    def remote(source, target, send_sem, recv_sem, device):
        return pltpu.make_async_remote_copy(
            src_ref=source,
            dst_ref=target,
            send_sem=send_sem,
            recv_sem=recv_sem,
            device_id=device,
            device_id_type=pl.DeviceIdType.MESH,
        )

    def copy(group, c):
        source, target, device = (
            (x_ref.at[:, place(c, 1 - side), :], partner.at[:, span(c), :], at(0, 1 - side, 0)),
            (upper.at[1, :, span(c), :], halves.at[1, :, span(c), :], at(0, side, -1)),
            (lower.at[0, :, span(c), :], halves.at[2, :, span(c), :], at(-1, side, 0)),
            (upper.at[0, :, span(c), :], halves.at[3, :, span(c), :], at(-1, side, -1)),
        )[group]
        return remote(source, target, send.at[group, c], recv.at[group, c], device)

    def edge(group):
        source, device = (
            (lower.at[1], at(0, 1 - side, 0)),
            (upper.at[1], at(0, 1 - side, -1)),
            (lower.at[0], at(-1, 1 - side, 0)),
            (upper.at[0], at(-1, 1 - side, -1)),
        )[group]
        return remote(
            source.at[:, pl.ds(0, SLACK), :],
            halves.at[group, :, pl.ds(cols, SLACK), :],
            edge_send.at[group],
            edge_recv.at[group],
            device,
        )

    def give_back(kind, c, origin):
        frame, part = kind // 2, kind % 2
        device = at(1 - frame, frame, part)
        return remote(
            result.at[1 - frame, pl.ds(half * part, half), span(c), :],
            out_ref.at[pl.ds(half * (1 - part), half), place(c, origin), :],
            out_send.at[kind, c],
            out_recv.at[part, origin, c],
            device,
        )

    barrier = pltpu.get_barrier_semaphore()
    known = [
        at(i, to_side, j)
        for i in (-1, 0, 1)
        for j in (-1, 0, 1)
        for to_side in ((1 - side,) if (i, j) == (0, 0) else (side, 1 - side))
    ]
    for device in known:
        pl.semaphore_signal(
            barrier, inc=1, device_id=device, device_id_type=pl.DeviceIdType.MESH
        )
    wk[...] = jnp.zeros_like(wk)
    raw = (w_mut, w_slf, w_prj, w_gte, w_upp, w_dwn)
    ready = (wq, wk, wv, wpm, wps, wgu, wd)
    arrange_weights(0, *raw, *ready)
    pl.semaphore_wait(barrier, len(known))
    for c in range(chunks):
        copy(0, c).start()
    arrange_weights(1, *raw, *ready)

    @pl.loop(0, chunks)
    def _(c):
        copy(0, c).wait_recv()
        own, other = layer_result(
            x_ref[:, place(c, side), :], partner[:, span(c), :], 0, *ready
        )
        upper[side, :, span(c), :] = own[:half]
        lower[side, :, span(c), :] = own[half:]
        upper[1 - side, :, span(c), :] = other[:half]
        lower[1 - side, :, span(c), :] = other[half:]
        for group in (2, 3, 1):
            copy(group, c).start()
        halves[0, :, span(c), :] = lower[1, :, span(c), :]

        @pl.when(c == 0)
        def _():
            for group in range(4):
                edge(group).start()

    for group in (2, 3, 1):
        copy(group, 0).wait_recv()

    def shifted(top, bottom, c):
        joined = jnp.concatenate(
            [halves[top, :, span(c, wide), :], halves[bottom, :, span(c, wide), :]], axis=0
        )
        return joined.astype(f32)[:, half : half + CHUNK, :]

    @pl.loop(0, chunks)
    def _(c):
        @pl.when(c < chunks - 1)
        def _():
            for group in (2, 3, 1):
                copy(group, c + 1).wait_recv()

        @pl.when(c == chunks - 1)
        def _():
            for group in range(4):
                edge(group).wait_recv()

        odd, even = layer_result(shifted(0, 1, c), shifted(2, 3, c), 1, *ready)
        result[0, :, span(c), :] = odd
        result[1, :, span(c), :] = even
        give_back(0, c, side).start()
        give_back(1, c, side).start()
        give_back(3, c, side).start()

        @pl.when(side == 0)
        def _():
            give_back(2, c, side).start()

        @pl.when(side == 1)
        def _():
            out_ref[half:, place(c, 1), :] = odd[:half]

    for c in range(chunks):
        give_back(0, c, 0).wait_recv()
        give_back(1, c, 0).wait_recv()
        give_back(1, c, 1).wait_recv()
        for kind in (0, 1, 3):
            give_back(kind, c, side).wait_send()
        for group in range(4):
            copy(group, c).wait_send()

    @pl.when(side == 0)
    def _():
        for c in range(chunks):
            give_back(0, c, 1).wait_recv()
            give_back(2, c, 0).wait_send()

    for group in range(4):
        edge(group).wait_send()


def on_device(features, w_mutual, w_self, w_proj, w_gate, w_up, w_down):
    half = WIN // 2
    current = features[0].transpose(1, 2, 0)
    cols = current.shape[1] // 2
    chunks = cols // CHUNK
    in_vmem = pl.BlockSpec(memory_space=pltpu.VMEM)
    result = pl.pallas_call(
        both_layers,
        in_specs=[in_vmem] * 7,
        out_specs=in_vmem,
        out_shape=jax.ShapeDtypeStruct(current.shape, bf16),
        scratch_shapes=[
            pltpu.VMEM((WIN, cols, C), bf16),
            pltpu.VMEM((2, half, cols, C), bf16),
            pltpu.VMEM((2, half, cols, C), bf16),
            pltpu.VMEM((4, half, cols + SLACK, C), bf16),
            pltpu.VMEM((2, WIN, cols, C), bf16),
            pltpu.VMEM((2, 2 * LANES, C), bf16),
            pltpu.VMEM((2, C, 2 * LANES), bf16),
            pltpu.VMEM((2, 2 * VROWS, C), bf16),
            pltpu.VMEM((2, C, C), bf16),
            pltpu.VMEM((2, C, C), bf16),
            pltpu.VMEM((2, 2 * FFN, C), bf16),
            pltpu.VMEM((2, C, FFN), bf16),
            pltpu.SemaphoreType.DMA((4, chunks)),
            pltpu.SemaphoreType.DMA((4, chunks)),
            pltpu.SemaphoreType.DMA((4,)),
            pltpu.SemaphoreType.DMA((4,)),
            pltpu.SemaphoreType.DMA((4, chunks)),
            pltpu.SemaphoreType.DMA((2, 2, chunks)),
        ],
        compiler_params=pltpu.CompilerParams(
            vmem_limit_bytes=48 * 1024 * 1024, collective_id=0, has_side_effects=True
        ),
        cost_estimate=pl.CostEstimate(
            flops=2_400_000_000, bytes_accessed=3_000_000, transcendentals=6_000_000
        ),
    )(current, w_mutual, w_self, w_proj, w_gate, w_up, w_down)
    return jnp.roll(result, half, axis=1).transpose(2, 0, 1)[None]


def solution(mesh):
    in_specs = (P("frame", None, "strip", None), P(), P(), P(), P(), P(), P())
    out_specs = P("frame", None, "strip", None)
    return jax.shard_map(
        on_device, mesh=mesh, in_specs=in_specs, out_specs=out_specs, check_vma=False
    )
```

```python
import math

import jax
import jax.numpy as jnp
from jax import lax
from jax.experimental import pallas as pl
from jax.experimental.pallas import tpu as pltpu
from jax.sharding import PartitionSpec as P

C = 120
HEADS = 6
HEAD = 20
FFN = 240
WIN = 8
TOK = WIN * WIN
LANES = 128
PAIR = 2 * HEAD
GROUP = 48
VROWS = 3 * GROUP
CHUNK = 32
SLACK = 16
epsilon = 1e-05
f32 = jnp.float32
bf16 = jnp.bfloat16


def nn(a, b):
    return lax.dot_general(a, b, (((1,), (0,)), ((), ())), preferred_element_type=f32)


def nt(a, b):
    return lax.dot_general(a, b, (((1,), (1,)), ((), ())), preferred_element_type=f32)


def normed(values, axis):
    centred = values - jnp.mean(values, axis=axis, keepdims=True)
    spread = jnp.mean(centred * centred, axis=axis, keepdims=True)
    return (centred * lax.rsqrt(spread + epsilon)).astype(bf16)


def window_tokens(block):
    wins = block.shape[1] // WIN
    shaped = block.astype(f32).reshape(WIN, wins, WIN, C)
    return shaped.transpose(1, 0, 2, 3).reshape(wins * TOK, C)


def gelu(values):
    return 0.5 * values * (1.0 + lax.erf(values * (0.5 ** 0.5)))


def layer_chunk(x_tok, wq, wk, wv, wpm, wps, wgu, wd):
    tokens = x_tok.shape[0]
    normal = normed(x_tok, 1)
    q_t = nt(wq, normal)
    keys = nn(normal, wk).astype(bf16)
    values = nt(wv, normal)
    pairs = tokens // LANES

    low = lax.broadcasted_iota(jnp.int32, (1, LANES), 1) < TOK
    row = lax.broadcasted_iota(jnp.int32, (LANES, LANES), 0)
    lane = lax.broadcasted_iota(jnp.int32, (LANES, LANES), 1)
    head_of = jnp.where(lane < TOK, 0, 1)
    masks = jnp.concatenate(
        [
            ((row >= PAIR * j + HEAD * head_of) & (row < PAIR * j + HEAD * head_of + HEAD))
            .astype(f32).astype(bf16)
            for j in range(3)
        ],
        axis=1,
    )
    first_head = lax.broadcasted_iota(jnp.int32, (C, LANES), 0) % PAIR < HEAD
    factor = HEAD ** (-0.5) * math.log2(math.e)

    def block_diagonal(first, second):
        right = jnp.zeros((first.shape[0], second.shape[1]), bf16)
        left = jnp.zeros((second.shape[0], first.shape[1]), bf16)
        return jnp.concatenate(
            [
                jnp.concatenate([first, right], axis=1),
                jnp.concatenate([left, second], axis=1),
            ],
            axis=0,
        )

    def spread(query):
        return jnp.concatenate([query.astype(bf16)] * 3, axis=1) * masks

    def score(own, mate, q_self, q_mut):
        self_keys = jnp.concatenate([keys[own, LANES:], keys[mate, LANES:]], axis=0)
        return nn(
            block_diagonal(self_keys, keys[mate, :LANES]),
            jnp.concatenate([spread(q_self), spread(q_mut)], axis=0),
        )

    def soften(scores):
        top = jnp.max(scores, axis=0, keepdims=True)
        weights = jnp.exp2((scores - top) * factor)
        return (weights * (1.0 / jnp.sum(weights, axis=0, keepdims=True))).astype(bf16)

    def soften_both(scores):
        return jnp.concatenate([soften(scores[: 2 * TOK]), soften(scores[2 * TOK :])], axis=0)

    def gather(v_self, v_mut, weights):
        parts = [
            nn(
                block_diagonal(
                    v_self[GROUP * j : GROUP * (j + 1)], v_mut[GROUP * j : GROUP * (j + 1)]
                ),
                weights[:, LANES * j : LANES * (j + 1)],
            )
            for j in range(3)
        ]
        selfish = jnp.concatenate([part[:PAIR] for part in parts], axis=0)
        return selfish, jnp.concatenate([part[GROUP : GROUP + PAIR] for part in parts], axis=0)

    def swap(block):
        return pltpu.roll(block, TOK, 1)

    def merge(first, second):
        return jnp.where(
            first_head,
            jnp.where(low, first, swap(second)),
            jnp.where(low, swap(first), second),
        ).astype(bf16)

    def scores_of(pair):
        mate = (pair + pairs // 2) % pairs
        cols = slice(LANES * pair, LANES * (pair + 1))
        own_a = slice(LANES * pair, LANES * pair + TOK)
        own_b = slice(LANES * pair + TOK, LANES * (pair + 1))
        mate_a = slice(LANES * mate, LANES * mate + TOK)
        mate_b = slice(LANES * mate + TOK, LANES * (mate + 1))
        q_m, q_s = q_t[:LANES, cols], q_t[LANES:, cols]
        q_m_r, q_s_r = swap(q_m), swap(q_s)
        return [
            score(own_a, mate_a, jnp.where(low, q_s, q_s_r), jnp.where(low, q_m, q_m_r)),
            score(own_b, mate_b, jnp.where(low, q_s_r, q_s), jnp.where(low, q_m_r, q_m)),
        ]

    def mixed(pair, weights):
        mate = (pair + pairs // 2) % pairs
        cols = slice(LANES * pair, LANES * (pair + 1))
        mate_cols = slice(LANES * mate, LANES * (mate + 1))
        v_own, v_m, v_s = values[VROWS:, cols], values[:VROWS, mate_cols], values[VROWS:, mate_cols]
        self_a, mut_a = gather(
            jnp.where(low, v_own, swap(v_s)).astype(bf16), v_m[:, :TOK].astype(bf16), weights[0]
        )
        self_b, mut_b = gather(
            jnp.where(low, swap(v_own), v_s).astype(bf16),
            swap(v_m)[:, :TOK].astype(bf16),
            weights[1],
        )
        return merge(mut_a, mut_b), merge(self_a, self_b)

    scores, weights, mutual, selfish = {}, {}, [], []
    for step in range(pairs + 2):
        if step < pairs:
            scores[step] = scores_of(step)
        if 0 <= step - 1 < pairs:
            weights[step - 1] = [soften_both(one) for one in scores.pop(step - 1)]
        if step >= 2:
            first, second = mixed(step - 2, weights.pop(step - 2))
            mutual.append(first)
            selfish.append(second)
    mutual = jnp.concatenate(mutual, axis=1)
    selfish = jnp.concatenate(selfish, axis=1)

    eye = (
        lax.broadcasted_iota(jnp.int32, (C, C), 0) == lax.broadcasted_iota(jnp.int32, (C, C), 1)
    ).astype(f32).astype(bf16)
    middle = nt(eye, x_tok.astype(bf16)) + (nn(wpm, mutual) + nn(wps, selfish))
    second = normed(middle, 0)
    gate_up = nn(wgu, second)
    hidden = (gelu(gate_up[:FFN]) * gate_up[FFN:]).astype(bf16)
    return middle + nn(wd, hidden)


def layer_result(first, second, layer, wq, wk, wv, wpm, wps, wgu, wd):
    tokens = jnp.concatenate([window_tokens(first), window_tokens(second)], axis=0)
    result = layer_chunk(
        tokens, wq[layer], wk[layer], wv[layer], wpm[layer], wps[layer], wgu[layer], wd[layer]
    )
    wins = CHUNK // WIN
    back = result.T.reshape(2, wins, WIN, WIN, C).transpose(0, 2, 1, 3, 4)
    back = back.reshape(2, WIN, CHUNK, C).astype(bf16)
    return back[0], back[1]


def arrange_weights(layer, w_mut, w_slf, w_prj, w_gte, w_upp, w_dwn, wq, wk, wv, wpm, wps, wgu, wd):
    blank = jnp.zeros((LANES - C, C), f32)
    for part, source in enumerate((w_mut, w_slf)):
        whole = source[layer].astype(f32)
        turned = whole.T
        wq[layer, LANES * part : LANES * (part + 1)] = jnp.concatenate(
            [turned[:C], blank], axis=0
        ).astype(bf16)
        wk[layer, :, LANES * part : LANES * part + C] = whole[:, C : 2 * C].astype(bf16)
        rows = []
        for j in range(3):
            rows += [turned[2 * C + PAIR * j : 2 * C + PAIR * (j + 1)], blank]
        wv[layer, VROWS * part : VROWS * (part + 1)] = jnp.concatenate(rows, axis=0).astype(bf16)
    joint = w_prj[layer].astype(f32)
    wpm[layer] = joint[:C].T.astype(bf16)
    wps[layer] = joint[C:].T.astype(bf16)
    wgu[layer, :FFN] = w_gte[layer].astype(f32).T.astype(bf16)
    wgu[layer, FFN:] = w_upp[layer].astype(f32).T.astype(bf16)
    wd[layer] = w_dwn[layer].astype(f32).T.astype(bf16)


def both_layers(
    x_ref, w_mut, w_slf, w_prj, w_gte, w_upp, w_dwn, out_ref,
    partner, upper, lower, halves, result,
    wq, wk, wv, wpm, wps, wgu, wd,
    send, recv, edge_send, edge_recv, out_send, out_recv,
):
    half = WIN // 2
    cols = x_ref.shape[1] // 2
    chunks = cols // CHUNK
    wide = CHUNK + SLACK
    couples, strips = lax.axis_size("frame") // 2, lax.axis_size("strip")
    f, s = lax.axis_index("frame"), lax.axis_index("strip")
    side = lax.rem(f, 2)
    couple = lax.div(f, 2)

    def at(d_couple, to_side, d_strip):
        to_couple = lax.rem(couple + d_couple + couples, couples)
        return (2 * to_couple + to_side, lax.rem(s + d_strip + strips, strips))

    def span(c, width=CHUNK):
        return pl.ds(pl.multiple_of(c * CHUNK, CHUNK), width)

    def place(c, which):
        return pl.ds(pl.multiple_of(which * cols + c * CHUNK, CHUNK), CHUNK)

    def remote(source, target, send_sem, recv_sem, device):
        return pltpu.make_async_remote_copy(
            src_ref=source,
            dst_ref=target,
            send_sem=send_sem,
            recv_sem=recv_sem,
            device_id=device,
            device_id_type=pl.DeviceIdType.MESH,
        )

    ahead = 1 - 2 * side

    def copy(group, c):
        source, target, device = (
            (x_ref.at[:, place(c, 1 - side), :], partner.at[:, span(c), :], at(0, 1 - side, 0)),
            (upper.at[0, :, span(c), :], halves.at[1, :, span(c), :], at(0, side, -1)),
            (lower.at[1, :, span(c), :], halves.at[2, :, span(c), :], at(ahead, side, 0)),
            (upper.at[1, :, span(c), :], halves.at[3, :, span(c), :], at(ahead, side, -1)),
        )[group]
        return remote(source, target, send.at[group, c], recv.at[group, c], device)

    def edge(group):
        source, device = (
            (lower.at[1], at(0, 1 - side, 0)),
            (upper.at[1], at(0, 1 - side, -1)),
            (lower.at[0], at(-ahead, 1 - side, 0)),
            (upper.at[0], at(-ahead, 1 - side, -1)),
        )[group]
        return remote(
            source.at[:, pl.ds(0, SLACK), :],
            halves.at[group, :, pl.ds(cols, SLACK), :],
            edge_send.at[group],
            edge_recv.at[group],
            device,
        )

    def give_back(kind, c):
        frame, part, device = (
            (1, 0, at(-ahead, 1 - side, 0)),
            (1, 1, at(-ahead, 1 - side, 1)),
            (0, 1, at(0, side, 1)),
        )[kind]
        return remote(
            result.at[frame, pl.ds(half * part, half), span(c), :],
            out_ref.at[pl.ds(half * (1 - part), half), place(c, side), :],
            out_send.at[kind, c],
            out_recv.at[kind, c],
            device,
        )

    barrier = pltpu.get_barrier_semaphore()
    known = [
        at(i, to_side, j)
        for i in (-1, 0, 1)
        for j in (-1, 0, 1)
        for to_side in ((1 - side,) if (i, j) == (0, 0) else (side, 1 - side))
    ]
    for device in known:
        pl.semaphore_signal(
            barrier, inc=1, device_id=device, device_id_type=pl.DeviceIdType.MESH
        )
    wk[...] = jnp.zeros_like(wk)
    raw = (w_mut, w_slf, w_prj, w_gte, w_upp, w_dwn)
    ready = (wq, wk, wv, wpm, wps, wgu, wd)
    arrange_weights(0, *raw, *ready)
    pl.semaphore_wait(barrier, len(known))
    for c in range(chunks):
        copy(0, c).start()
    arrange_weights(1, *raw, *ready)

    @pl.loop(0, chunks)
    def _(c):
        copy(0, c).wait_recv()
        own, other = layer_result(
            x_ref[:, place(c, side), :], partner[:, span(c), :], 0, *ready
        )
        upper[0, :, span(c), :] = own[:half]
        lower[0, :, span(c), :] = own[half:]
        upper[1, :, span(c), :] = other[:half]
        lower[1, :, span(c), :] = other[half:]
        for group in (2, 3, 1):
            copy(group, c).start()
        halves[0, :, span(c), :] = own[half:]

        @pl.when(c == 0)
        def _():
            for group in range(4):
                edge(group).start()

    for group in (2, 3, 1):
        copy(group, 0).wait_recv()

    def shifted(top, bottom, c):
        joined = jnp.concatenate(
            [halves[top, :, span(c, wide), :], halves[bottom, :, span(c, wide), :]], axis=0
        )
        return joined.astype(f32)[:, half : half + CHUNK, :]

    @pl.loop(0, chunks)
    def _(c):
        @pl.when(c < chunks - 1)
        def _():
            for group in (2, 3, 1):
                copy(group, c + 1).wait_recv()

        @pl.when(c == chunks - 1)
        def _():
            for group in range(4):
                edge(group).wait_recv()

        own, other = layer_result(shifted(0, 1, c), shifted(2, 3, c), 1, *ready)
        result[0, :, span(c), :] = own
        result[1, :, span(c), :] = other
        out_ref[half:, place(c, side), :] = own[:half]
        for kind in range(3):
            give_back(kind, c).start()

    for c in range(chunks):
        for kind in range(3):
            give_back(kind, c).wait()
        for group in range(4):
            copy(group, c).wait_send()

    for group in range(4):
        edge(group).wait_send()


def on_device(features, w_mutual, w_self, w_proj, w_gate, w_up, w_down):
    half = WIN // 2
    current = features[0].transpose(1, 2, 0)
    cols = current.shape[1] // 2
    chunks = cols // CHUNK
    in_vmem = pl.BlockSpec(memory_space=pltpu.VMEM)
    result = pl.pallas_call(
        both_layers,
        in_specs=[in_vmem] * 7,
        out_specs=in_vmem,
        out_shape=jax.ShapeDtypeStruct(current.shape, bf16),
        scratch_shapes=[
            pltpu.VMEM((WIN, cols, C), bf16),
            pltpu.VMEM((2, half, cols, C), bf16),
            pltpu.VMEM((2, half, cols, C), bf16),
            pltpu.VMEM((4, half, cols + SLACK, C), bf16),
            pltpu.VMEM((2, WIN, cols, C), bf16),
            pltpu.VMEM((2, 2 * LANES, C), bf16),
            pltpu.VMEM((2, C, 2 * LANES), bf16),
            pltpu.VMEM((2, 2 * VROWS, C), bf16),
            pltpu.VMEM((2, C, C), bf16),
            pltpu.VMEM((2, C, C), bf16),
            pltpu.VMEM((2, 2 * FFN, C), bf16),
            pltpu.VMEM((2, C, FFN), bf16),
            pltpu.SemaphoreType.DMA((4, chunks)),
            pltpu.SemaphoreType.DMA((4, chunks)),
            pltpu.SemaphoreType.DMA((4,)),
            pltpu.SemaphoreType.DMA((4,)),
            pltpu.SemaphoreType.DMA((3, chunks)),
            pltpu.SemaphoreType.DMA((3, chunks)),
        ],
        compiler_params=pltpu.CompilerParams(
            vmem_limit_bytes=48 * 1024 * 1024, collective_id=0, has_side_effects=True
        ),
        cost_estimate=pl.CostEstimate(
            flops=2_400_000_000, bytes_accessed=3_000_000, transcendentals=6_000_000
        ),
    )(current, w_mutual, w_self, w_proj, w_gate, w_up, w_down)
    return jnp.roll(result, half, axis=1).transpose(2, 0, 1)[None]


def solution(mesh):
    in_specs = (P("frame", None, "strip", None), P(), P(), P(), P(), P(), P())
    out_specs = P("frame", None, "strip", None)
    return jax.shard_map(
        on_device, mesh=mesh, in_specs=in_specs, out_specs=out_specs, check_vma=False
    )
```

```python
import math

import jax
import jax.numpy as jnp
from jax import lax
from jax.experimental import pallas as pl
from jax.experimental.pallas import tpu as pltpu
from jax.sharding import PartitionSpec as P

C = 120
HEADS = 6
HEAD = 20
FFN = 240
WIN = 8
TOK = WIN * WIN
LANES = 128
PAIR = 2 * HEAD
GROUP = 48
VROWS = 3 * GROUP
CHUNK = 32
SLACK = 16
epsilon = 1e-05
f32 = jnp.float32
bf16 = jnp.bfloat16


def nn(a, b):
    return lax.dot_general(a, b, (((1,), (0,)), ((), ())), preferred_element_type=f32)


def nt(a, b):
    return lax.dot_general(a, b, (((1,), (1,)), ((), ())), preferred_element_type=f32)


def normed(values, axis):
    centred = values - jnp.mean(values, axis=axis, keepdims=True)
    spread = jnp.mean(centred * centred, axis=axis, keepdims=True)
    return (centred * lax.rsqrt(spread + epsilon)).astype(bf16)


def window_tokens(block):
    wins = block.shape[1] // WIN
    shaped = block.astype(f32).reshape(WIN, wins, WIN, C)
    return shaped.transpose(1, 0, 2, 3).reshape(wins * TOK, C)


def gelu(values):
    return 0.5 * values * (1.0 + lax.erf(values * (0.5 ** 0.5)))


def layer_chunk(x_tok, wq, wk, wv, wpm, wps, wgu, wd):
    tokens = x_tok.shape[0]
    normal = normed(x_tok, 1)
    q_t = nt(wq, normal)
    keys = nn(normal, wk).astype(bf16)
    values = nt(wv, normal)
    pairs = tokens // LANES

    low = lax.broadcasted_iota(jnp.int32, (1, LANES), 1) < TOK
    row = lax.broadcasted_iota(jnp.int32, (LANES, LANES), 0)
    lane = lax.broadcasted_iota(jnp.int32, (LANES, LANES), 1)
    head_of = jnp.where(lane < TOK, 0, 1)
    masks = jnp.concatenate(
        [
            ((row >= PAIR * j + HEAD * head_of) & (row < PAIR * j + HEAD * head_of + HEAD))
            .astype(f32).astype(bf16)
            for j in range(3)
        ],
        axis=1,
    )
    first_head = lax.broadcasted_iota(jnp.int32, (C, LANES), 0) % PAIR < HEAD
    factor = HEAD ** (-0.5) * math.log2(math.e)

    def block_diagonal(first, second):
        right = jnp.zeros((first.shape[0], second.shape[1]), bf16)
        left = jnp.zeros((second.shape[0], first.shape[1]), bf16)
        return jnp.concatenate(
            [
                jnp.concatenate([first, right], axis=1),
                jnp.concatenate([left, second], axis=1),
            ],
            axis=0,
        )

    def spread(query):
        return jnp.concatenate([query.astype(bf16)] * 3, axis=1) * masks

    def score(own, mate, q_self, q_mut):
        self_keys = jnp.concatenate([keys[own, LANES:], keys[mate, LANES:]], axis=0)
        return nn(
            block_diagonal(self_keys, keys[mate, :LANES]),
            jnp.concatenate([spread(q_self), spread(q_mut)], axis=0),
        )

    def soften(scores):
        top = jnp.max(scores, axis=0, keepdims=True)
        weights = jnp.exp2((scores - top) * factor)
        return (weights * (1.0 / jnp.sum(weights, axis=0, keepdims=True))).astype(bf16)

    def soften_both(scores):
        return jnp.concatenate([soften(scores[: 2 * TOK]), soften(scores[2 * TOK :])], axis=0)

    def gather(v_self, v_mut, weights):
        parts = [
            nn(
                block_diagonal(
                    v_self[GROUP * j : GROUP * (j + 1)], v_mut[GROUP * j : GROUP * (j + 1)]
                ),
                weights[:, LANES * j : LANES * (j + 1)],
            )
            for j in range(3)
        ]
        selfish = jnp.concatenate([part[:PAIR] for part in parts], axis=0)
        return selfish, jnp.concatenate([part[GROUP : GROUP + PAIR] for part in parts], axis=0)

    def swap(block):
        return pltpu.roll(block, TOK, 1)

    def merge(first, second):
        return jnp.where(
            first_head,
            jnp.where(low, first, swap(second)),
            jnp.where(low, swap(first), second),
        ).astype(bf16)

    def scores_of(pair):
        mate = (pair + pairs // 2) % pairs
        cols = slice(LANES * pair, LANES * (pair + 1))
        own_a = slice(LANES * pair, LANES * pair + TOK)
        own_b = slice(LANES * pair + TOK, LANES * (pair + 1))
        mate_a = slice(LANES * mate, LANES * mate + TOK)
        mate_b = slice(LANES * mate + TOK, LANES * (mate + 1))
        q_m, q_s = q_t[:LANES, cols], q_t[LANES:, cols]
        q_m_r, q_s_r = swap(q_m), swap(q_s)
        return [
            score(own_a, mate_a, jnp.where(low, q_s, q_s_r), jnp.where(low, q_m, q_m_r)),
            score(own_b, mate_b, jnp.where(low, q_s_r, q_s), jnp.where(low, q_m_r, q_m)),
        ]

    def mixed(pair, weights):
        mate = (pair + pairs // 2) % pairs
        cols = slice(LANES * pair, LANES * (pair + 1))
        mate_cols = slice(LANES * mate, LANES * (mate + 1))
        v_own, v_m, v_s = values[VROWS:, cols], values[:VROWS, mate_cols], values[VROWS:, mate_cols]
        self_a, mut_a = gather(
            jnp.where(low, v_own, swap(v_s)).astype(bf16), v_m[:, :TOK].astype(bf16), weights[0]
        )
        self_b, mut_b = gather(
            jnp.where(low, swap(v_own), v_s).astype(bf16),
            swap(v_m)[:, :TOK].astype(bf16),
            weights[1],
        )
        return merge(mut_a, mut_b), merge(self_a, self_b)

    scores, weights, mutual, selfish = {}, {}, [], []
    for step in range(pairs + 2):
        if step < pairs:
            scores[step] = scores_of(step)
        if 0 <= step - 1 < pairs:
            weights[step - 1] = [soften_both(one) for one in scores.pop(step - 1)]
        if step >= 2:
            first, second = mixed(step - 2, weights.pop(step - 2))
            mutual.append(first)
            selfish.append(second)
    mutual = jnp.concatenate(mutual, axis=1)
    selfish = jnp.concatenate(selfish, axis=1)

    eye = (
        lax.broadcasted_iota(jnp.int32, (C, C), 0) == lax.broadcasted_iota(jnp.int32, (C, C), 1)
    ).astype(f32).astype(bf16)
    middle = nt(eye, x_tok.astype(bf16)) + (nn(wpm, mutual) + nn(wps, selfish))
    second = normed(middle, 0)
    gate_up = nn(wgu, second)
    hidden = (gelu(gate_up[:FFN]) * gate_up[FFN:]).astype(bf16)
    return middle + nn(wd, hidden)


def layer_result(first, second, layer, wq, wk, wv, wpm, wps, wgu, wd):
    tokens = jnp.concatenate([window_tokens(first), window_tokens(second)], axis=0)
    result = layer_chunk(
        tokens, wq[layer], wk[layer], wv[layer], wpm[layer], wps[layer], wgu[layer], wd[layer]
    )
    wins = CHUNK // WIN
    back = result.T.reshape(2, wins, WIN, WIN, C).transpose(0, 2, 1, 3, 4)
    back = back.reshape(2, WIN, CHUNK, C).astype(bf16)
    return back[0], back[1]


def arrange_weights(layer, w_mut, w_slf, w_prj, w_gte, w_upp, w_dwn, wq, wk, wv, wpm, wps, wgu, wd):
    blank = jnp.zeros((LANES - C, C), f32)
    for part, source in enumerate((w_mut, w_slf)):
        whole = source[layer].astype(f32)
        turned = whole.T
        wq[layer, LANES * part : LANES * (part + 1)] = jnp.concatenate(
            [turned[:C], blank], axis=0
        ).astype(bf16)
        wk[layer, :, LANES * part : LANES * part + C] = whole[:, C : 2 * C].astype(bf16)
        rows = []
        for j in range(3):
            rows += [turned[2 * C + PAIR * j : 2 * C + PAIR * (j + 1)], blank]
        wv[layer, VROWS * part : VROWS * (part + 1)] = jnp.concatenate(rows, axis=0).astype(bf16)
    joint = w_prj[layer].astype(f32)
    wpm[layer] = joint[:C].T.astype(bf16)
    wps[layer] = joint[C:].T.astype(bf16)
    wgu[layer, :FFN] = w_gte[layer].astype(f32).T.astype(bf16)
    wgu[layer, FFN:] = w_upp[layer].astype(f32).T.astype(bf16)
    wd[layer] = w_dwn[layer].astype(f32).T.astype(bf16)


def both_layers(
    x_ref, w_mut, w_slf, w_prj, w_gte, w_upp, w_dwn, out_ref,
    partner, upper, lower, halves, result,
    wq, wk, wv, wpm, wps, wgu, wd,
    send, recv, edge_send, edge_recv, out_send, out_recv,
):
    half = WIN // 2
    cols = x_ref.shape[1] // 2
    chunks = cols // CHUNK
    wide = CHUNK + SLACK
    couples, strips = lax.axis_size("frame") // 2, lax.axis_size("strip")
    f, s = lax.axis_index("frame"), lax.axis_index("strip")
    side = lax.rem(f, 2)
    couple = lax.div(f, 2)

    def at(d_couple, to_side, d_strip):
        to_couple = lax.rem(couple + d_couple + couples, couples)
        return (2 * to_couple + to_side, lax.rem(s + d_strip + strips, strips))

    def span(c, width=CHUNK):
        return pl.ds(pl.multiple_of(c * CHUNK, CHUNK), width)

    def place(c, which):
        return pl.ds(pl.multiple_of(which * cols + c * CHUNK, CHUNK), CHUNK)

    def remote(source, target, send_sem, recv_sem, device):
        return pltpu.make_async_remote_copy(
            src_ref=source,
            dst_ref=target,
            send_sem=send_sem,
            recv_sem=recv_sem,
            device_id=device,
            device_id_type=pl.DeviceIdType.MESH,
        )

    ahead = 1 - 2 * side

    def copy(group, c):
        source, target, device = (
            (x_ref.at[:, place(c, 1 - side), :], partner.at[:, span(c), :], at(0, 1 - side, 0)),
            (upper.at[0, :, span(c), :], halves.at[1, :, span(c), :], at(0, side, -1)),
            (lower.at[1, :, span(c), :], halves.at[2, :, span(c), :], at(ahead, side, 0)),
            (upper.at[1, :, span(c), :], halves.at[3, :, span(c), :], at(ahead, side, -1)),
        )[group]
        return remote(source, target, send.at[group, c], recv.at[group, c], device)

    def edge(group):
        source, device = (
            (lower.at[1], at(0, 1 - side, 0)),
            (upper.at[1], at(0, 1 - side, -1)),
            (lower.at[0], at(-ahead, 1 - side, 0)),
            (upper.at[0], at(-ahead, 1 - side, -1)),
        )[group]
        return remote(
            source.at[:, pl.ds(0, SLACK), :],
            halves.at[group, :, pl.ds(cols, SLACK), :],
            edge_send.at[group],
            edge_recv.at[group],
            device,
        )

    def give_back(kind, c):
        frame, part, device = (
            (1, 0, at(-ahead, 1 - side, 0)),
            (1, 1, at(-ahead, 1 - side, 1)),
            (0, 1, at(0, side, 1)),
        )[kind]
        return remote(
            result.at[frame, pl.ds(half * part, half), span(c), :],
            out_ref.at[pl.ds(half * (1 - part), half), place(c, side), :],
            out_send.at[kind, c],
            out_recv.at[kind, c],
            device,
        )

    barrier = pltpu.get_barrier_semaphore()
    known = [
        at(i, to_side, j)
        for i in (-1, 0, 1)
        for j in (-1, 0, 1)
        for to_side in ((1 - side,) if (i, j) == (0, 0) else (side, 1 - side))
    ]
    for device in known:
        pl.semaphore_signal(
            barrier, inc=1, device_id=device, device_id_type=pl.DeviceIdType.MESH
        )
    pl.semaphore_wait(barrier, len(known))
    copy(0, 0).start()
    wk[...] = jnp.zeros_like(wk)
    raw = (w_mut, w_slf, w_prj, w_gte, w_upp, w_dwn)
    ready = (wq, wk, wv, wpm, wps, wgu, wd)
    arrange_weights(0, *raw, *ready)
    copy(0, 1).start()
    arrange_weights(1, *raw, *ready)

    @pl.loop(0, chunks)
    def _(c):
        copy(0, c).wait_recv()

        @pl.when(c + 2 < chunks)
        def _():
            copy(0, c + 2).start()

        own, other = layer_result(
            x_ref[:, place(c, side), :], partner[:, span(c), :], 0, *ready
        )
        upper[0, :, span(c), :] = own[:half]
        lower[0, :, span(c), :] = own[half:]
        upper[1, :, span(c), :] = other[:half]
        lower[1, :, span(c), :] = other[half:]
        for group in (2, 3, 1):
            copy(group, c).start()
        halves[0, :, span(c), :] = own[half:]

        @pl.when(c == 0)
        def _():
            for group in range(4):
                edge(group).start()

    for group in (2, 3, 1):
        copy(group, 0).wait_recv()

    def shifted(top, bottom, c):
        joined = jnp.concatenate(
            [halves[top, :, span(c, wide), :], halves[bottom, :, span(c, wide), :]], axis=0
        )
        return joined.astype(f32)[:, half : half + CHUNK, :]

    @pl.loop(0, chunks)
    def _(c):
        @pl.when(c < chunks - 1)
        def _():
            for group in (2, 3, 1):
                copy(group, c + 1).wait_recv()

        @pl.when(c == chunks - 1)
        def _():
            for group in range(4):
                edge(group).wait_recv()

        own, other = layer_result(shifted(0, 1, c), shifted(2, 3, c), 1, *ready)
        result[0, :, span(c), :] = own
        result[1, :, span(c), :] = other
        out_ref[half:, place(c, side), :] = own[:half]
        for kind in range(3):
            give_back(kind, c).start()

    for c in range(chunks):
        for kind in range(3):
            give_back(kind, c).wait()
        for group in range(4):
            copy(group, c).wait_send()

    for group in range(4):
        edge(group).wait_send()


def on_device(features, w_mutual, w_self, w_proj, w_gate, w_up, w_down):
    half = WIN // 2
    current = features[0].transpose(1, 2, 0)
    cols = current.shape[1] // 2
    chunks = cols // CHUNK
    in_vmem = pl.BlockSpec(memory_space=pltpu.VMEM)
    result = pl.pallas_call(
        both_layers,
        in_specs=[in_vmem] * 7,
        out_specs=in_vmem,
        out_shape=jax.ShapeDtypeStruct(current.shape, bf16),
        scratch_shapes=[
            pltpu.VMEM((WIN, cols, C), bf16),
            pltpu.VMEM((2, half, cols, C), bf16),
            pltpu.VMEM((2, half, cols, C), bf16),
            pltpu.VMEM((4, half, cols + SLACK, C), bf16),
            pltpu.VMEM((2, WIN, cols, C), bf16),
            pltpu.VMEM((2, 2 * LANES, C), bf16),
            pltpu.VMEM((2, C, 2 * LANES), bf16),
            pltpu.VMEM((2, 2 * VROWS, C), bf16),
            pltpu.VMEM((2, C, C), bf16),
            pltpu.VMEM((2, C, C), bf16),
            pltpu.VMEM((2, 2 * FFN, C), bf16),
            pltpu.VMEM((2, C, FFN), bf16),
            pltpu.SemaphoreType.DMA((4, chunks)),
            pltpu.SemaphoreType.DMA((4, chunks)),
            pltpu.SemaphoreType.DMA((4,)),
            pltpu.SemaphoreType.DMA((4,)),
            pltpu.SemaphoreType.DMA((3, chunks)),
            pltpu.SemaphoreType.DMA((3, chunks)),
        ],
        compiler_params=pltpu.CompilerParams(
            vmem_limit_bytes=48 * 1024 * 1024, collective_id=0, has_side_effects=True
        ),
        cost_estimate=pl.CostEstimate(
            flops=2_400_000_000, bytes_accessed=3_000_000, transcendentals=6_000_000
        ),
    )(current, w_mutual, w_self, w_proj, w_gate, w_up, w_down)
    return jnp.roll(result, half, axis=1).transpose(2, 0, 1)[None]


def solution(mesh):
    in_specs = (P("frame", None, "strip", None), P(), P(), P(), P(), P(), P())
    out_specs = P("frame", None, "strip", None)
    return jax.shard_map(
        on_device, mesh=mesh, in_specs=in_specs, out_specs=out_specs, check_vma=False
    )
```

```python
import math

import jax
import jax.numpy as jnp
from jax import lax
from jax.experimental import pallas as pl
from jax.experimental.pallas import tpu as pltpu
from jax.sharding import PartitionSpec as P

C = 120
HEADS = 6
HEAD = 20
FFN = 240
WIN = 8
TOK = WIN * WIN
LANES = 128
PAIR = 2 * HEAD
GROUP = 48
VROWS = 3 * GROUP
CHUNK = 64
SLACK = 16
epsilon = 1e-05
f32 = jnp.float32
bf16 = jnp.bfloat16


def nn(a, b):
    return lax.dot_general(a, b, (((1,), (0,)), ((), ())), preferred_element_type=f32)


def nt(a, b):
    return lax.dot_general(a, b, (((1,), (1,)), ((), ())), preferred_element_type=f32)


def normed(values, axis):
    centred = values - jnp.mean(values, axis=axis, keepdims=True)
    spread = jnp.mean(centred * centred, axis=axis, keepdims=True)
    return (centred * lax.rsqrt(spread + epsilon)).astype(bf16)


def window_tokens(block):
    wins = block.shape[1] // WIN
    shaped = block.astype(f32).reshape(WIN, wins, WIN, C)
    return shaped.transpose(1, 0, 2, 3).reshape(wins * TOK, C)


def gelu(values):
    return 0.5 * values * (1.0 + lax.erf(values * (0.5 ** 0.5)))


def layer_chunk(x_tok, wq, wk, wv, wpm, wps, wgu, wd):
    tokens = x_tok.shape[0]
    normal = normed(x_tok, 1)
    q_t = nt(wq, normal)
    keys = nn(normal, wk).astype(bf16)
    values = nt(wv, normal)
    pairs = tokens // LANES

    low = lax.broadcasted_iota(jnp.int32, (1, LANES), 1) < TOK
    row = lax.broadcasted_iota(jnp.int32, (LANES, LANES), 0)
    lane = lax.broadcasted_iota(jnp.int32, (LANES, LANES), 1)
    head_of = jnp.where(lane < TOK, 0, 1)
    masks = jnp.concatenate(
        [
            ((row >= PAIR * j + HEAD * head_of) & (row < PAIR * j + HEAD * head_of + HEAD))
            .astype(f32).astype(bf16)
            for j in range(3)
        ],
        axis=1,
    )
    first_head = lax.broadcasted_iota(jnp.int32, (C, LANES), 0) % PAIR < HEAD
    factor = HEAD ** (-0.5) * math.log2(math.e)

    def block_diagonal(first, second):
        right = jnp.zeros((first.shape[0], second.shape[1]), bf16)
        left = jnp.zeros((second.shape[0], first.shape[1]), bf16)
        return jnp.concatenate(
            [
                jnp.concatenate([first, right], axis=1),
                jnp.concatenate([left, second], axis=1),
            ],
            axis=0,
        )

    def spread(query):
        return jnp.concatenate([query.astype(bf16)] * 3, axis=1) * masks

    def score(own, mate, q_self, q_mut):
        self_keys = jnp.concatenate([keys[own, LANES:], keys[mate, LANES:]], axis=0)
        return nn(
            block_diagonal(self_keys, keys[mate, :LANES]),
            jnp.concatenate([spread(q_self), spread(q_mut)], axis=0),
        )

    def soften(scores):
        top = jnp.max(scores, axis=0, keepdims=True)
        weights = jnp.exp2((scores - top) * factor)
        return (weights * (1.0 / jnp.sum(weights, axis=0, keepdims=True))).astype(bf16)

    def soften_both(scores):
        return jnp.concatenate([soften(scores[: 2 * TOK]), soften(scores[2 * TOK :])], axis=0)

    def gather(v_self, v_mut, weights):
        parts = [
            nn(
                block_diagonal(
                    v_self[GROUP * j : GROUP * (j + 1)], v_mut[GROUP * j : GROUP * (j + 1)]
                ),
                weights[:, LANES * j : LANES * (j + 1)],
            )
            for j in range(3)
        ]
        selfish = jnp.concatenate([part[:PAIR] for part in parts], axis=0)
        return selfish, jnp.concatenate([part[GROUP : GROUP + PAIR] for part in parts], axis=0)

    def swap(block):
        return pltpu.roll(block, TOK, 1)

    def merge(first, second):
        return jnp.where(
            first_head,
            jnp.where(low, first, swap(second)),
            jnp.where(low, swap(first), second),
        ).astype(bf16)

    def scores_of(pair):
        mate = (pair + pairs // 2) % pairs
        cols = slice(LANES * pair, LANES * (pair + 1))
        own_a = slice(LANES * pair, LANES * pair + TOK)
        own_b = slice(LANES * pair + TOK, LANES * (pair + 1))
        mate_a = slice(LANES * mate, LANES * mate + TOK)
        mate_b = slice(LANES * mate + TOK, LANES * (mate + 1))
        q_m, q_s = q_t[:LANES, cols], q_t[LANES:, cols]
        q_m_r, q_s_r = swap(q_m), swap(q_s)
        return [
            score(own_a, mate_a, jnp.where(low, q_s, q_s_r), jnp.where(low, q_m, q_m_r)),
            score(own_b, mate_b, jnp.where(low, q_s_r, q_s), jnp.where(low, q_m_r, q_m)),
        ]

    def mixed(pair, weights):
        mate = (pair + pairs // 2) % pairs
        cols = slice(LANES * pair, LANES * (pair + 1))
        mate_cols = slice(LANES * mate, LANES * (mate + 1))
        v_own, v_m, v_s = values[VROWS:, cols], values[:VROWS, mate_cols], values[VROWS:, mate_cols]
        self_a, mut_a = gather(
            jnp.where(low, v_own, swap(v_s)).astype(bf16), v_m[:, :TOK].astype(bf16), weights[0]
        )
        self_b, mut_b = gather(
            jnp.where(low, swap(v_own), v_s).astype(bf16),
            swap(v_m)[:, :TOK].astype(bf16),
            weights[1],
        )
        return merge(mut_a, mut_b), merge(self_a, self_b)

    scores, weights, mutual, selfish = {}, {}, [], []
    for step in range(pairs + 2):
        if step < pairs:
            scores[step] = scores_of(step)
        if 0 <= step - 1 < pairs:
            weights[step - 1] = [soften_both(one) for one in scores.pop(step - 1)]
        if step >= 2:
            first, second = mixed(step - 2, weights.pop(step - 2))
            mutual.append(first)
            selfish.append(second)
    mutual = jnp.concatenate(mutual, axis=1)
    selfish = jnp.concatenate(selfish, axis=1)

    eye = (
        lax.broadcasted_iota(jnp.int32, (C, C), 0) == lax.broadcasted_iota(jnp.int32, (C, C), 1)
    ).astype(f32).astype(bf16)
    middle = nt(eye, x_tok.astype(bf16)) + (nn(wpm, mutual) + nn(wps, selfish))
    second = normed(middle, 0)
    gate_up = nn(wgu, second)
    hidden = (gelu(gate_up[:FFN]) * gate_up[FFN:]).astype(bf16)
    return middle + nn(wd, hidden)


def layer_result(first, second, layer, wq, wk, wv, wpm, wps, wgu, wd):
    tokens = jnp.concatenate([window_tokens(first), window_tokens(second)], axis=0)
    result = layer_chunk(
        tokens, wq[layer], wk[layer], wv[layer], wpm[layer], wps[layer], wgu[layer], wd[layer]
    )
    wins = CHUNK // WIN
    back = result.T.reshape(2, wins, WIN, WIN, C).transpose(0, 2, 1, 3, 4)
    back = back.reshape(2, WIN, CHUNK, C).astype(bf16)
    return back[0], back[1]


def arrange_weights(layer, w_mut, w_slf, w_prj, w_gte, w_upp, w_dwn, wq, wk, wv, wpm, wps, wgu, wd):
    blank = jnp.zeros((LANES - C, C), f32)
    for part, source in enumerate((w_mut, w_slf)):
        whole = source[layer].astype(f32)
        turned = whole.T
        wq[layer, LANES * part : LANES * (part + 1)] = jnp.concatenate(
            [turned[:C], blank], axis=0
        ).astype(bf16)
        wk[layer, :, LANES * part : LANES * part + C] = whole[:, C : 2 * C].astype(bf16)
        rows = []
        for j in range(3):
            rows += [turned[2 * C + PAIR * j : 2 * C + PAIR * (j + 1)], blank]
        wv[layer, VROWS * part : VROWS * (part + 1)] = jnp.concatenate(rows, axis=0).astype(bf16)
    joint = w_prj[layer].astype(f32)
    wpm[layer] = joint[:C].T.astype(bf16)
    wps[layer] = joint[C:].T.astype(bf16)
    wgu[layer, :FFN] = w_gte[layer].astype(f32).T.astype(bf16)
    wgu[layer, FFN:] = w_upp[layer].astype(f32).T.astype(bf16)
    wd[layer] = w_dwn[layer].astype(f32).T.astype(bf16)


def both_layers(
    x_ref, w_mut, w_slf, w_prj, w_gte, w_upp, w_dwn, out_ref,
    partner, upper, lower, halves, result,
    wq, wk, wv, wpm, wps, wgu, wd,
    send, recv, edge_send, edge_recv, out_send, out_recv,
):
    half = WIN // 2
    cols = x_ref.shape[1] // 2
    chunks = cols // CHUNK
    wide = CHUNK + SLACK
    couples, strips = lax.axis_size("frame") // 2, lax.axis_size("strip")
    f, s = lax.axis_index("frame"), lax.axis_index("strip")
    side = lax.rem(f, 2)
    couple = lax.div(f, 2)

    def at(d_couple, to_side, d_strip):
        to_couple = lax.rem(couple + d_couple + couples, couples)
        return (2 * to_couple + to_side, lax.rem(s + d_strip + strips, strips))

    def span(c, width=CHUNK):
        return pl.ds(pl.multiple_of(c * CHUNK, CHUNK), width)

    def place(c, which):
        return pl.ds(pl.multiple_of(which * cols + c * CHUNK, CHUNK), CHUNK)

    def remote(source, target, send_sem, recv_sem, device):
        return pltpu.make_async_remote_copy(
            src_ref=source,
            dst_ref=target,
            send_sem=send_sem,
            recv_sem=recv_sem,
            device_id=device,
            device_id_type=pl.DeviceIdType.MESH,
        )

    ahead = 1 - 2 * side

    def copy(group, c):
        source, target, device = (
            (x_ref.at[:, place(c, 1 - side), :], partner.at[:, span(c), :], at(0, 1 - side, 0)),
            (upper.at[0, :, span(c), :], halves.at[1, :, span(c), :], at(0, side, -1)),
            (lower.at[1, :, span(c), :], halves.at[2, :, span(c), :], at(ahead, side, 0)),
            (upper.at[1, :, span(c), :], halves.at[3, :, span(c), :], at(ahead, side, -1)),
        )[group]
        return remote(source, target, send.at[group, c], recv.at[group, c], device)

    def edge(group):
        source, device = (
            (lower.at[1], at(0, 1 - side, 0)),
            (upper.at[1], at(0, 1 - side, -1)),
            (lower.at[0], at(-ahead, 1 - side, 0)),
            (upper.at[0], at(-ahead, 1 - side, -1)),
        )[group]
        return remote(
            source.at[:, pl.ds(0, SLACK), :],
            halves.at[group, :, pl.ds(cols, SLACK), :],
            edge_send.at[group],
            edge_recv.at[group],
            device,
        )

    def give_back(kind, c):
        frame, part, device = (
            (1, 0, at(-ahead, 1 - side, 0)),
            (1, 1, at(-ahead, 1 - side, 1)),
            (0, 1, at(0, side, 1)),
        )[kind]
        return remote(
            result.at[frame, pl.ds(half * part, half), span(c), :],
            out_ref.at[pl.ds(half * (1 - part), half), place(c, side), :],
            out_send.at[kind, c],
            out_recv.at[kind, c],
            device,
        )

    barrier = pltpu.get_barrier_semaphore()
    known = [
        at(i, to_side, j)
        for i in (-1, 0, 1)
        for j in (-1, 0, 1)
        for to_side in ((1 - side,) if (i, j) == (0, 0) else (side, 1 - side))
    ]
    for device in known:
        pl.semaphore_signal(
            barrier, inc=1, device_id=device, device_id_type=pl.DeviceIdType.MESH
        )
    pl.semaphore_wait(barrier, len(known))
    copy(0, 0).start()
    wk[...] = jnp.zeros_like(wk)
    raw = (w_mut, w_slf, w_prj, w_gte, w_upp, w_dwn)
    ready = (wq, wk, wv, wpm, wps, wgu, wd)
    arrange_weights(0, *raw, *ready)
    copy(0, 1).start()
    arrange_weights(1, *raw, *ready)

    @pl.loop(0, chunks)
    def _(c):
        copy(0, c).wait_recv()

        @pl.when(c + 2 < chunks)
        def _():
            copy(0, c + 2).start()

        own, other = layer_result(
            x_ref[:, place(c, side), :], partner[:, span(c), :], 0, *ready
        )
        upper[0, :, span(c), :] = own[:half]
        lower[0, :, span(c), :] = own[half:]
        upper[1, :, span(c), :] = other[:half]
        lower[1, :, span(c), :] = other[half:]
        for group in (2, 3, 1):
            copy(group, c).start()
        halves[0, :, span(c), :] = own[half:]

        @pl.when(c == 0)
        def _():
            for group in range(4):
                edge(group).start()

    for group in (2, 3, 1):
        copy(group, 0).wait_recv()

    def shifted(top, bottom, c):
        joined = jnp.concatenate(
            [halves[top, :, span(c, wide), :], halves[bottom, :, span(c, wide), :]], axis=0
        )
        return joined.astype(f32)[:, half : half + CHUNK, :]

    @pl.loop(0, chunks)
    def _(c):
        @pl.when(c < chunks - 1)
        def _():
            for group in (2, 3, 1):
                copy(group, c + 1).wait_recv()

        @pl.when(c == chunks - 1)
        def _():
            for group in range(4):
                edge(group).wait_recv()

        own, other = layer_result(shifted(0, 1, c), shifted(2, 3, c), 1, *ready)
        result[0, :, span(c), :] = own
        result[1, :, span(c), :] = other
        out_ref[half:, place(c, side), :] = own[:half]
        for kind in range(3):
            give_back(kind, c).start()

    for c in range(chunks):
        for kind in range(3):
            give_back(kind, c).wait()
        for group in range(4):
            copy(group, c).wait_send()

    for group in range(4):
        edge(group).wait_send()


def on_device(features, w_mutual, w_self, w_proj, w_gate, w_up, w_down):
    half = WIN // 2
    current = features[0].transpose(1, 2, 0)
    cols = current.shape[1] // 2
    chunks = cols // CHUNK
    in_vmem = pl.BlockSpec(memory_space=pltpu.VMEM)
    result = pl.pallas_call(
        both_layers,
        in_specs=[in_vmem] * 7,
        out_specs=in_vmem,
        out_shape=jax.ShapeDtypeStruct(current.shape, bf16),
        scratch_shapes=[
            pltpu.VMEM((WIN, cols, C), bf16),
            pltpu.VMEM((2, half, cols, C), bf16),
            pltpu.VMEM((2, half, cols, C), bf16),
            pltpu.VMEM((4, half, cols + SLACK, C), bf16),
            pltpu.VMEM((2, WIN, cols, C), bf16),
            pltpu.VMEM((2, 2 * LANES, C), bf16),
            pltpu.VMEM((2, C, 2 * LANES), bf16),
            pltpu.VMEM((2, 2 * VROWS, C), bf16),
            pltpu.VMEM((2, C, C), bf16),
            pltpu.VMEM((2, C, C), bf16),
            pltpu.VMEM((2, 2 * FFN, C), bf16),
            pltpu.VMEM((2, C, FFN), bf16),
            pltpu.SemaphoreType.DMA((4, chunks)),
            pltpu.SemaphoreType.DMA((4, chunks)),
            pltpu.SemaphoreType.DMA((4,)),
            pltpu.SemaphoreType.DMA((4,)),
            pltpu.SemaphoreType.DMA((3, chunks)),
            pltpu.SemaphoreType.DMA((3, chunks)),
        ],
        compiler_params=pltpu.CompilerParams(
            vmem_limit_bytes=48 * 1024 * 1024, collective_id=0, has_side_effects=True
        ),
        cost_estimate=pl.CostEstimate(
            flops=2_400_000_000, bytes_accessed=3_000_000, transcendentals=6_000_000
        ),
    )(current, w_mutual, w_self, w_proj, w_gate, w_up, w_down)
    return jnp.roll(result, half, axis=1).transpose(2, 0, 1)[None]


def solution(mesh):
    in_specs = (P("frame", None, "strip", None), P(), P(), P(), P(), P(), P())
    out_specs = P("frame", None, "strip", None)
    return jax.shard_map(
        on_device, mesh=mesh, in_specs=in_specs, out_specs=out_specs, check_vma=False
    )
```
